128 devices in a mesh: row: 8 (over z_hi, y), col: 16 (over z_lo, x, core).
Axes of the slice: x: 4, y: 4, z: 4 (z_hi: 2, z_lo: 2; z = z_hi * 2 + z_lo), core: 2. Of those that a mesh axis runs over, the one named last changes fastest.
Arguments:
- inputs: bfloat16 [1536, 7168], P('col', 'row'), may hold values from -6 to 6
- teacher: bfloat16 [1536, 7168], P('col', 'row'), may hold values from -6 to 6
- weight_in: bfloat16 [7168, 18432], P('row', 'col'), may hold values from -0.0625 to 0.0625
- weight_out: bfloat16 [18432, 7168], P('col', 'row'), may hold values from -0.046875 to 0.046875
Outputs:
- grad_inputs: bfloat16 [1536, 7168], P('col', 'row')
- grad_weight_in: bfloat16 [7168, 18432], P('row', 'col')
- grad_weight_out: bfloat16 [18432, 7168], P('col', 'row')
The draws below stay inside these ranges and needn't reach their ends.
All inputs are finite; a program needn't handle non-finite values.
Results may differ from the reference program's by a relative error of at most 0.008.
Values may be sent and summed in bfloat16 or wider, within the bound.
A program may use at most 128 MiB of HBM per device.

```python
import math
import jax
import jax.numpy as jnp

D = 7168
FF = 18432
TOKENS = 1536


def level_of(rng, dims, cuts, smallest, high):
    def one(axis_at, blocks):
        heights = jax.random.uniform(jax.random.fold_in(jax.random.fold_in(rng, 6), axis_at), (blocks,), jnp.float32, smallest / len(cuts), high / len(cuts))
        return jnp.repeat(jnp.exp(heights), dims[axis_at] // blocks).reshape((-1,) + (1,) * (len(dims) - axis_at - 1))

    loudness = one(*cuts[0])
    for cut in cuts[1:]:
        loudness = loudness * one(*cut)
    return loudness


def bell_draw(own_key, shape, scale, limit, pieces=(), kind=jnp.bfloat16):
    loudness = level_of(own_key, shape, pieces, -0.22, 0.18) if pieces else 1.0
    array = jax.random.normal(own_key, shape, jnp.float32) * scale * loudness
    return jnp.minimum(jnp.maximum(array, -limit), limit).astype(kind)


def setup_inputs(seed: int = 0) -> dict:
    arg_keys = jax.random.split(jax.random.key(seed), 5)
    inputs = bell_draw(arg_keys[0], (TOKENS, D), 1.0, 6.0, ((0, 16), (1, 8)))
    teacher = bell_draw(arg_keys[1], (TOKENS, D), 1.0, 6.0, ((0, 16), (1, 8)))
    weight_in = bell_draw(arg_keys[2], (D, FF), D ** -0.5, 0.0625, ((0, 8), (1, 16)))
    weight_out = bell_draw(arg_keys[3], (FF, D), FF ** -0.5, 0.046875, ((0, 16), (1, 8)))
    return dict(inputs=inputs, teacher=teacher, weight_in=weight_in, weight_out=weight_out)


def gelu_value(hidden):
    return 0.5 * hidden * (1.0 + jax.scipy.special.erf(hidden / math.sqrt(2.0)))

def gelu_slope(hidden):
    cumul = 0.5 * (1.0 + jax.scipy.special.erf(hidden / math.sqrt(2.0)))
    return cumul + hidden * jnp.exp(-0.5 * hidden * hidden) / math.sqrt(2.0 * math.pi)

def reference(inputs, teacher, weight_in, weight_out):
    hidden = jnp.dot(inputs, weight_in, preferred_element_type=jnp.float32)
    act = gelu_value(hidden).astype(jnp.bfloat16)
    student = jnp.dot(act, weight_out, preferred_element_type=jnp.float32)
    d_out = (0.125 * (student - teacher.astype(jnp.float32))).astype(jnp.bfloat16)
    grad_weight_out = jnp.dot(act.T, d_out, preferred_element_type=jnp.float32).astype(jnp.bfloat16)
    d_act = jnp.dot(d_out, weight_out.T, preferred_element_type=jnp.float32)
    d_hidden = (d_act * gelu_slope(hidden)).astype(jnp.bfloat16)
    grad_weight_in = jnp.dot(inputs.T, d_hidden, preferred_element_type=jnp.float32).astype(jnp.bfloat16)
    grad_inputs = jnp.dot(d_hidden, weight_in.T, preferred_element_type=jnp.float32).astype(jnp.bfloat16)
    return (grad_inputs, grad_weight_in, grad_weight_out)
```

```python
import math

import jax
import jax.numpy as jnp
from jax import lax
from jax.experimental import pallas as pl
from jax.experimental.pallas import tpu as pltpu
from jax.sharding import PartitionSpec as P

MESH = pl.DeviceIdType.MESH
F32 = jnp.float32
BF16 = jnp.bfloat16

K = 2
RB = 96 // K
D = 896
H = 1152
HALF = 8 * RB

ORDER = (
    "A0", "B0", "A1", "B1", "A2", "B2", "A3", "B3", "A4", "A5",
    "A6", "B4", "A7", "B5", "B6", "A8", "B7", "A9", "B8", "B9",
    "A10", "G", "B10", "A11", "B11", "A12", "A13", "A14", "B12", "A15",
    "B13", "W", "B14", "B15",
)


def gelu_value(hidden):
    return 0.5 * hidden * (1.0 + lax.erf(hidden * (1.0 / math.sqrt(2.0))))


def gelu_slope(hidden):
    cumul = 0.5 * (1.0 + lax.erf(hidden * (1.0 / math.sqrt(2.0))))
    return cumul + hidden * jnp.exp(-0.5 * hidden * hidden) * (1.0 / math.sqrt(2.0 * math.pi))


def kernel(
    x_hbm, t_hbm, wi_hbm, wo_hbm, gi_hbm, gwi_hbm, gwo_hbm,
    wi, wo, tch, gi, gwi, gwo, hid,
    hp, hz, hy, hz2, hy2, ag, xg, sp, sc, sr,
    lsem, osem, cs, cr, ccs, ccr, rs, rr, gs, gr, ss, sr_sem, scs, scr,
):
    r, c = lax.axis_index("row"), lax.axis_index("col")
    zh, y = r // 4, r % 4
    chip, core = c // 2, c % 2
    oz, oc = 1 - zh, 1 - core
    ys = [(y + j) % 4 for j in (1, 2, 3)]
    chips = [(chip + j) % 8 for j in range(1, 8)]
    y_dev = [(zh * 4 + v, c) for v in ys]
    z_dev = (oz * 4 + y, c)
    chip_dev = [(r, v * 2 + core) for v in chips]
    core_dev = (r, chip * 2 + oc)

    def send(src, dst, ssem, rsem, dev):
        pltpu.make_async_remote_copy(
            src_ref=src, dst_ref=dst, send_sem=ssem, recv_sem=rsem, device_id=dev, device_id_type=MESH
        ).start()

    def await_bytes(like, sem):
        pltpu.make_async_copy(like, like, sem).wait()

    loads = [pltpu.make_async_copy(x_hbm.at[pl.ds(k * RB, RB)], xg.at[0, k, core, chip], lsem.at[k]) for k in range(K)]
    load_wi = pltpu.make_async_copy(wi_hbm, wi, lsem.at[K])
    load_wo = pltpu.make_async_copy(wo_hbm, wo, lsem.at[K + 1])
    load_t = pltpu.make_async_copy(t_hbm, tch, lsem.at[K + 2])
    for load in loads:
        load.start()

    barrier = pltpu.get_barrier_semaphore()
    peers = y_dev + [z_dev] + chip_dev + [core_dev]
    for peer in peers:
        pl.semaphore_signal(barrier, inc=1, device_id=peer, device_id_type=MESH)
    pl.semaphore_wait(barrier, len(peers))

    def gather_col_start(q, k):
        for dev in chip_dev:
            own = xg.at[q, k, core, chip]
            send(own, own, cs.at[q, k], cr.at[q, k], dev)

    def gather_col_mid(q, k):
        await_bytes(sr.at[q, k], cr.at[q, k])
        send(xg.at[q, k, core], xg.at[q, k, core], ccs.at[q, k], ccr.at[q, k], core_dev)

    def gather_col_end(q, k):
        await_bytes(sc.at[q, k], ccr.at[q, k])

    def product(out, left, right, transposed):
        depth = left.shape[-1]
        a = left[...].reshape(HALF, depth)
        if transposed:
            res = lax.dot_general(a, right[...], (((1,), (1,)), ((), ())), preferred_element_type=F32)
        else:
            res = jnp.dot(a, right[...], preferred_element_type=F32)
        out[...] = res.astype(BF16).reshape(out.shape)

    def row_start(q, k):
        weights, transposed = (wi, False) if q == 0 else (wo, True)
        product(hp.at[q, k, 1], xg.at[q, k, 1], weights, transposed)
        send(hp.at[q, k, 1, oz], hz.at[q, k], rs.at[q, k, 0], rr.at[q, k, 0], z_dev)
        product(hp.at[q, k, 0], xg.at[q, k, 0], weights, transposed)
        for j in (1, 0, 2):
            send(hp.at[q, k, 0, :, ys[j]], hy.at[q, k, j], rs.at[q, k, 1], rr.at[q, k, 1], y_dev[j])

    def row_mid(q, k):
        await_bytes(hz.at[q, k], rr.at[q, k, 0])
        hp[q, k, 1, zh] = (hp[q, k, 1, zh].astype(F32) + hz[q, k].astype(F32)).astype(BF16)
        for j in (1, 0, 2):
            send(hp.at[q, k, 1, zh, ys[j]], hy2.at[q, k, j], rs.at[q, k, 2], rr.at[q, k, 2], y_dev[j])
        await_bytes(hy.at[q, k], rr.at[q, k, 1])
        total = hp[q, k, 0, oz, y].astype(F32)
        for j in range(3):
            total = total + hy[q, k, j, oz].astype(F32)
        hp[q, k, 0, oz, y] = total.astype(BF16)
        send(hp.at[q, k, 0, oz, y], hz2.at[q, k], rs.at[q, k, 3], rr.at[q, k, 3], z_dev)

    def activate(q, k, part, total):
        if q == 0:
            hid[k, part] = total
            value = gelu_value(total)
        else:
            value = total * gelu_slope(hid[k, part])
        ag[q, k, part, zh, y] = value.astype(BF16)

    def row_end(q, k):
        await_bytes(hz2.at[q, k], rr.at[q, k, 3])
        total = hp[q, k, 0, zh, y].astype(F32) + hz2[q, k].astype(F32)
        for j in range(3):
            total = total + hy[q, k, j, zh].astype(F32)
        activate(q, k, 0, total)
        own = ag.at[q, k, 0, zh, y]
        send(own, own, gs.at[q, k, 0], gr.at[q, k, 0], z_dev)
        for j in (1, 0, 2):
            send(own, own, gs.at[q, k, 1], gr.at[q, k, 1], y_dev[j])
        await_bytes(hy2.at[q, k], rr.at[q, k, 2])
        total = hp[q, k, 1, zh, y].astype(F32)
        for j in range(3):
            total = total + hy2[q, k, j].astype(F32)
        activate(q, k, 1, total)
        own = ag.at[q, k, 1, zh, y]
        for j in (1, 0, 2):
            send(own, own, gs.at[q, k, 2], gr.at[q, k, 2], y_dev[j])
        send(own, own, gs.at[q, k, 3], gr.at[q, k, 3], z_dev)

    def gather_row_mid(q, k):
        await_bytes(hz2.at[q, k], gr.at[q, k, 0])
        for j in (1, 0, 2):
            got = ag.at[q, k, 0, oz, y]
            send(got, got, gs.at[q, k, 1], gr.at[q, k, 1], y_dev[j])
        await_bytes(hy2.at[q, k], gr.at[q, k, 2])
        for j in range(3):
            got = ag.at[q, k, 1, zh, ys[j]]
            send(got, got, gs.at[q, k, 3], gr.at[q, k, 3], z_dev)

    def col_start(q, k):
        await_bytes(hy.at[q, k], gr.at[q, k, 1])
        await_bytes(hz.at[q, k], gr.at[q, k, 3])
        weights, transposed = (wo, False) if q == 0 else (wi, True)
        product(sp.at[q, k, oc], ag.at[q, k, oc], weights, transposed)
        send(sp.at[q, k, oc], sc.at[q, k], scs.at[q, k], scr.at[q, k], core_dev)
        product(sp.at[q, k, core], ag.at[q, k, core], weights, transposed)

    def col_mid(q, k):
        await_bytes(sc.at[q, k], scr.at[q, k])
        sp[q, k, core] = (sp[q, k, core].astype(F32) + sc[q, k].astype(F32)).astype(BF16)
        for j, dev in enumerate(chip_dev):
            send(sp.at[q, k, core, chips[j]], sr.at[q, k, j], ss.at[q, k], sr_sem.at[q, k], dev)

    def col_end(q, k):
        await_bytes(sr.at[q, k], sr_sem.at[q, k])
        total = sp[q, k, core, chip].astype(F32)
        for j in range(7):
            total = total + sr[q, k, j].astype(F32)
        rows = pl.ds(k * RB, RB)
        if q == 0:
            xg[1, k, core, chip] = (0.125 * (total - tch[rows, :].astype(F32))).astype(BF16)
            gather_col_start(1, k)
        else:
            gi[rows, :] = total.astype(BF16)
            pltpu.make_async_copy(gi.at[rows], gi_hbm.at[rows], osem.at[2 + k]).start()

    def weight_grad(out, left, right, tile):
        b = right.reshape(K * 2 * HALF, right.shape[-1])
        a = left.reshape(K * 2 * HALF, left.shape[-1])

        def step(i, carry):
            at = pl.ds(pl.multiple_of(i * tile, tile), tile)
            out[at, :] = lax.dot_general(
                a[:, at], b[...], (((0,), (0,)), ((), ())), preferred_element_type=F32
            ).astype(BF16)
            return carry

        lax.fori_loop(0, out.shape[0] // tile, step, 0)

    for k in range(K):
        loads[k].wait()
        gather_col_start(0, k)
    load_wi.start()
    load_wo.start()
    load_t.start()

    for event in ORDER:
        k, e = ord(event[0]) - ord("A"), event[1:]
        if event == "G":
            weight_grad(gwo, ag.at[0], xg.at[1], 384)
            pltpu.make_async_copy(gwo, gwo_hbm, osem.at[1]).start()
        elif event == "W":
            weight_grad(gwi, xg.at[0], ag.at[1], 128)
            pltpu.make_async_copy(gwi, gwi_hbm, osem.at[0]).start()
        elif e == "0":
            gather_col_mid(0, k)
        elif e == "1":
            if k == 0:
                load_wi.wait()
            gather_col_end(0, k)
            row_start(0, k)
        elif e == "2":
            row_mid(0, k)
        elif e == "3":
            row_end(0, k)
        elif e == "4":
            gather_row_mid(0, k)
        elif e == "5":
            if k == 0:
                load_wo.wait()
                load_t.wait()
            col_start(0, k)
        elif e == "6":
            col_mid(0, k)
        elif e == "7":
            col_end(0, k)
        elif e == "8":
            gather_col_mid(1, k)
        elif e == "9":
            gather_col_end(1, k)
            row_start(1, k)
        elif e == "10":
            row_mid(1, k)
        elif e == "11":
            row_end(1, k)
        elif e == "12":
            gather_row_mid(1, k)
        elif e == "13":
            col_start(1, k)
        elif e == "14":
            col_mid(1, k)
        elif e == "15":
            col_end(1, k)

    for q in range(2):
        for k in range(K):
            await_bytes(sr.at[q, k], cs.at[q, k])
            await_bytes(sc.at[q, k], ccs.at[q, k])
            await_bytes(hz.at[q, k], rs.at[q, k, 0])
            await_bytes(hy.at[q, k], rs.at[q, k, 1])
            await_bytes(hy2.at[q, k], rs.at[q, k, 2])
            await_bytes(hz2.at[q, k], rs.at[q, k, 3])
            await_bytes(hz2.at[q, k], gs.at[q, k, 0])
            await_bytes(hy.at[q, k], gs.at[q, k, 1])
            await_bytes(hy2.at[q, k], gs.at[q, k, 2])
            await_bytes(hz.at[q, k], gs.at[q, k, 3])
            await_bytes(sc.at[q, k], scs.at[q, k])
            await_bytes(sr.at[q, k], ss.at[q, k])
    pltpu.make_async_copy(gwi, gwi_hbm, osem.at[0]).wait()
    pltpu.make_async_copy(gwo, gwo_hbm, osem.at[1]).wait()
    for k in range(K):
        rows = pl.ds(k * RB, RB)
        pltpu.make_async_copy(gi.at[rows], gi_hbm.at[rows], osem.at[2 + k]).wait()


def shards(inputs, teacher, weight_in, weight_out):
    tokens = inputs.shape[0]
    dma = lambda *shape: pltpu.SemaphoreType.DMA(shape)
    scratch = [
        pltpu.VMEM((D, H), BF16),
        pltpu.VMEM((H, D), BF16),
        pltpu.VMEM((tokens, D), BF16),
        pltpu.VMEM((tokens, D), BF16),
        pltpu.VMEM((D, H), BF16),
        pltpu.VMEM((H, D), BF16),
        pltpu.VMEM((K, 2, RB, H), F32),
        pltpu.VMEM((2, K, 2, 2, 4, RB, H), BF16),
        pltpu.VMEM((2, K, 4, RB, H), BF16),
        pltpu.VMEM((2, K, 3, 2, RB, H), BF16),
        pltpu.VMEM((2, K, RB, H), BF16),
        pltpu.VMEM((2, K, 3, RB, H), BF16),
        pltpu.VMEM((2, K, 2, 2, 4, RB, H), BF16),
        pltpu.VMEM((2, K, 2, 8, RB, D), BF16),
        pltpu.VMEM((2, K, 2, 8, RB, D), BF16),
        pltpu.VMEM((2, K, 8, RB, D), BF16),
        pltpu.VMEM((2, K, 7, RB, D), BF16),
        dma(K + 3), dma(2 + K),
        dma(2, K), dma(2, K), dma(2, K), dma(2, K),
        dma(2, K, 4), dma(2, K, 4), dma(2, K, 4), dma(2, K, 4),
        dma(2, K), dma(2, K), dma(2, K), dma(2, K),
    ]
    anywhere = pl.BlockSpec(memory_space=pl.ANY)
    return pl.pallas_call(
        kernel,
        out_shape=(
            jax.ShapeDtypeStruct((tokens, D), BF16),
            jax.ShapeDtypeStruct((D, H), BF16),
            jax.ShapeDtypeStruct((H, D), BF16),
        ),
        in_specs=[anywhere] * 4,
        out_specs=(anywhere,) * 3,
        scratch_shapes=scratch,
        compiler_params=pltpu.CompilerParams(
            collective_id=0, has_side_effects=True, vmem_limit_bytes=58 * 1024 * 1024
        ),
    )(inputs, teacher, weight_in, weight_out)


def solution(mesh):
    placed = (P("col", "row"), P("col", "row"), P("row", "col"), P("col", "row"))
    return jax.shard_map(
        shards,
        mesh=mesh,
        in_specs=placed,
        out_specs=(P("col", "row"), P("row", "col"), P("col", "row")),
        check_vma=False,
    )
```

```python
import math

import jax
import jax.numpy as jnp
from jax import lax
from jax.experimental import pallas as pl
from jax.experimental.pallas import tpu as pltpu
from jax.sharding import PartitionSpec as P

MESH = pl.DeviceIdType.MESH
F32 = jnp.float32
BF16 = jnp.bfloat16

K = 3
RB = 96 // K
D = 896
H = 1152
HALF = 8 * RB

ORDER = (
    "A0gm", "A0gc", "B0gm", "C0gm", "A0rs", "B0gc", "C0gc", "B0rs", "A0rm", "A0re",
    "B0rm", "C0rs", "A0am", "B0re", "C0rm", "A0cs", "B0am", "A0cm", "C0re", "A0cz",
    "B0cs", "A0ce", "B0cm", "C0am", "C0cs", "A1gm", "B0cz", "B0ce", "A1gc", "C0cm",
    "B1gm", "A1rs", "B1gc", "C0cz", "A1rm", "B1rs", "C0ce", "C1gm", "A1re", "C1gc",
    "C1rs", "B1rm", "A1am", "B1re", "A1cs", "C1rm", "A1cm", "B1am", "C1re", "G",
    "B1cs", "A1cz", "C1am", "B1cm", "C1cs", "B1cz", "C1cm", "B1ce", "W", "C1cz",
    "A1ce", "C1ce",
)


def gelu_value(hidden):
    return 0.5 * hidden * (1.0 + lax.erf(hidden * (1.0 / math.sqrt(2.0))))


def gelu_slope(hidden):
    cumul = 0.5 * (1.0 + lax.erf(hidden * (1.0 / math.sqrt(2.0))))
    return cumul + hidden * jnp.exp(-0.5 * hidden * hidden) * (1.0 / math.sqrt(2.0 * math.pi))


def kernel(
    x_hbm, t_hbm, wi_hbm, wo_hbm, gi_hbm, gwi_hbm, gwo_hbm,
    wi, wo, tch, gi, gwi, gwo, hid,
    hp, hz, hy, hz2, hy2, ag, xg, sp, sc, sx, sz,
    lsem, osem, cs, cr, rs, rr, gs, gr, ss, st,
):
    r, c = lax.axis_index("row"), lax.axis_index("col")
    zh, y = r // 4, r % 4
    zl, x, core = c // 8, c // 2 % 4, c % 2
    oz, ol, oc = 1 - zh, 1 - zl, 1 - core
    ys = [(y + j) % 4 for j in (1, 2, 3)]
    xs = [(x + j) % 4 for j in (1, 2, 3)]
    y_dev = [(zh * 4 + v, c) for v in ys]
    z_dev = (oz * 4 + y, c)
    x_dev = [(r, zl * 8 + v * 2 + core) for v in xs]
    l_dev = (r, ol * 8 + x * 2 + core)
    core_dev = (r, zl * 8 + x * 2 + oc)

    def send(src, dst, ssem, rsem, dev):
        pltpu.make_async_remote_copy(
            src_ref=src, dst_ref=dst, send_sem=ssem, recv_sem=rsem, device_id=dev, device_id_type=MESH
        ).start()

    def await_bytes(like, sem):
        pltpu.make_async_copy(like, like, sem).wait()

    loads = [pltpu.make_async_copy(x_hbm.at[pl.ds(k * RB, RB)], xg.at[0, k, core, zl, x], lsem.at[k]) for k in range(K)]
    load_wi = pltpu.make_async_copy(wi_hbm, wi, lsem.at[K])
    load_wo = pltpu.make_async_copy(wo_hbm, wo, lsem.at[K + 1])
    load_t = pltpu.make_async_copy(t_hbm, tch, lsem.at[K + 2])
    for load in loads:
        load.start()

    barrier = pltpu.get_barrier_semaphore()
    peers = y_dev + x_dev + [z_dev, l_dev, core_dev]
    for peer in peers:
        pl.semaphore_signal(barrier, inc=1, device_id=peer, device_id_type=MESH)
    pl.semaphore_wait(barrier, len(peers))

    def gather_col_start(q, k):
        own = xg.at[q, k, core, zl, x]
        send(own, own, cs.at[q, k, 0], cr.at[q, k, 0], l_dev)
        for j in (1, 0, 2):
            send(own, own, cs.at[q, k, 1], cr.at[q, k, 1], x_dev[j])

    def gather_col_mid(q, k):
        await_bytes(sz.at[q, k], cr.at[q, k, 0])
        for j in (1, 0, 2):
            got = xg.at[q, k, core, ol, x]
            send(got, got, cs.at[q, k, 1], cr.at[q, k, 1], x_dev[j])

    def gather_col_core(q, k):
        await_bytes(sx.at[q, k], cr.at[q, k, 1])
        send(xg.at[q, k, core], xg.at[q, k, core], cs.at[q, k, 2], cr.at[q, k, 2], core_dev)

    def gather_col_end(q, k):
        await_bytes(sc.at[q, k], cr.at[q, k, 2])

    def product(out, left, right, transposed):
        depth = left.shape[-1]
        a = left[...].reshape(HALF, depth)
        if transposed:
            res = lax.dot_general(a, right[...], (((1,), (1,)), ((), ())), preferred_element_type=F32)
        else:
            res = jnp.dot(a, right[...], preferred_element_type=F32)
        out[...] = res.astype(BF16).reshape(out.shape)

    def row_start(q, k):
        weights, transposed = (wi, False) if q == 0 else (wo, True)
        product(hp.at[q, k, 1], xg.at[q, k, 1], weights, transposed)
        send(hp.at[q, k, 1, oz], hz.at[q, k], rs.at[q, k, 0], rr.at[q, k, 0], z_dev)
        product(hp.at[q, k, 0], xg.at[q, k, 0], weights, transposed)
        for j in (1, 0, 2):
            send(hp.at[q, k, 0, :, ys[j]], hy.at[q, k, j], rs.at[q, k, 1], rr.at[q, k, 1], y_dev[j])

    def row_mid(q, k):
        await_bytes(hz.at[q, k], rr.at[q, k, 0])
        hp[q, k, 1, zh] = (hp[q, k, 1, zh].astype(F32) + hz[q, k].astype(F32)).astype(BF16)
        for j in (1, 0, 2):
            send(hp.at[q, k, 1, zh, ys[j]], hy2.at[q, k, j], rs.at[q, k, 2], rr.at[q, k, 2], y_dev[j])
        await_bytes(hy.at[q, k], rr.at[q, k, 1])
        total = hp[q, k, 0, oz, y].astype(F32)
        for j in range(3):
            total = total + hy[q, k, j, oz].astype(F32)
        hp[q, k, 0, oz, y] = total.astype(BF16)
        send(hp.at[q, k, 0, oz, y], hz2.at[q, k], rs.at[q, k, 3], rr.at[q, k, 3], z_dev)

    def activate(q, k, part, total):
        if q == 0:
            hid[k, part] = total
            value = gelu_value(total)
        else:
            value = total * gelu_slope(hid[k, part])
        ag[q, k, part, zh, y] = value.astype(BF16)

    def row_end(q, k):
        await_bytes(hz2.at[q, k], rr.at[q, k, 3])
        total = hp[q, k, 0, zh, y].astype(F32) + hz2[q, k].astype(F32)
        for j in range(3):
            total = total + hy[q, k, j, zh].astype(F32)
        activate(q, k, 0, total)
        own = ag.at[q, k, 0, zh, y]
        send(own, own, gs.at[q, k, 0], gr.at[q, k, 0], z_dev)
        for j in (1, 0, 2):
            send(own, own, gs.at[q, k, 1], gr.at[q, k, 1], y_dev[j])
        await_bytes(hy2.at[q, k], rr.at[q, k, 2])
        total = hp[q, k, 1, zh, y].astype(F32)
        for j in range(3):
            total = total + hy2[q, k, j].astype(F32)
        activate(q, k, 1, total)
        own = ag.at[q, k, 1, zh, y]
        for j in (1, 0, 2):
            send(own, own, gs.at[q, k, 2], gr.at[q, k, 2], y_dev[j])
        send(own, own, gs.at[q, k, 3], gr.at[q, k, 3], z_dev)

    def gather_row_mid(q, k):
        await_bytes(hz2.at[q, k], gr.at[q, k, 0])
        for j in (1, 0, 2):
            got = ag.at[q, k, 0, oz, y]
            send(got, got, gs.at[q, k, 1], gr.at[q, k, 1], y_dev[j])
        await_bytes(hy2.at[q, k], gr.at[q, k, 2])
        for j in range(3):
            got = ag.at[q, k, 1, zh, ys[j]]
            send(got, got, gs.at[q, k, 3], gr.at[q, k, 3], z_dev)

    def col_start(q, k):
        await_bytes(hy.at[q, k], gr.at[q, k, 1])
        await_bytes(hz.at[q, k], gr.at[q, k, 3])
        weights, transposed = (wo, False) if q == 0 else (wi, True)
        product(sp.at[q, k, oc], ag.at[q, k, oc], weights, transposed)
        send(sp.at[q, k, oc], sc.at[q, k], ss.at[q, k, 0], st.at[q, k, 0], core_dev)
        product(sp.at[q, k, core], ag.at[q, k, core], weights, transposed)

    def col_mid(q, k):
        await_bytes(sc.at[q, k], st.at[q, k, 0])
        sp[q, k, core] = (sp[q, k, core].astype(F32) + sc[q, k].astype(F32)).astype(BF16)
        for j in (1, 0, 2):
            send(sp.at[q, k, core, :, xs[j]], sx.at[q, k, j], ss.at[q, k, 1], st.at[q, k, 1], x_dev[j])

    def col_z(q, k):
        await_bytes(sx.at[q, k], st.at[q, k, 1])
        total = sp[q, k, core, ol, x].astype(F32)
        for j in range(3):
            total = total + sx[q, k, j, ol].astype(F32)
        sp[q, k, core, ol, x] = total.astype(BF16)
        send(sp.at[q, k, core, ol, x], sz.at[q, k], ss.at[q, k, 2], st.at[q, k, 2], l_dev)

    def col_end(q, k):
        await_bytes(sz.at[q, k], st.at[q, k, 2])
        total = sp[q, k, core, zl, x].astype(F32) + sz[q, k].astype(F32)
        for j in range(3):
            total = total + sx[q, k, j, zl].astype(F32)
        rows = pl.ds(k * RB, RB)
        if q == 0:
            xg[1, k, core, zl, x] = (0.125 * (total - tch[rows, :].astype(F32))).astype(BF16)
            gather_col_start(1, k)
        else:
            gi[rows, :] = total.astype(BF16)
            pltpu.make_async_copy(gi.at[rows], gi_hbm.at[rows], osem.at[2 + k]).start()

    def weight_grad(out, left, right, tile):
        b = right.reshape(K * 2 * HALF, right.shape[-1])
        a = left.reshape(K * 2 * HALF, left.shape[-1])

        def step(i, carry):
            at = pl.ds(pl.multiple_of(i * tile, tile), tile)
            out[at, :] = lax.dot_general(
                a[:, at], b[...], (((0,), (0,)), ((), ())), preferred_element_type=F32
            ).astype(BF16)
            return carry

        lax.fori_loop(0, out.shape[0] // tile, step, 0)

    for k in range(K):
        loads[k].wait()
        gather_col_start(0, k)
    load_wi.start()
    load_wo.start()
    load_t.start()

    steps = {
        "gm": gather_col_mid, "gc": gather_col_core, "rm": row_mid, "re": row_end,
        "am": gather_row_mid, "cm": col_mid, "cz": col_z, "ce": col_end,
    }
    for event in ORDER:
        if event == "G":
            weight_grad(gwo, ag.at[0], xg.at[1], 384)
            pltpu.make_async_copy(gwo, gwo_hbm, osem.at[1]).start()
            continue
        if event == "W":
            weight_grad(gwi, xg.at[0], ag.at[1], 128)
            pltpu.make_async_copy(gwi, gwi_hbm, osem.at[0]).start()
            continue
        k, q, step = ord(event[0]) - ord("A"), int(event[1]), event[2:]
        if step == "rs":
            if event == "A0rs":
                load_wi.wait()
            gather_col_end(q, k)
            row_start(q, k)
        elif step == "cs":
            if event == "A0cs":
                load_wo.wait()
                load_t.wait()
            col_start(q, k)
        else:
            steps[step](q, k)

    for q in range(2):
        for k in range(K):
            await_bytes(sz.at[q, k], cs.at[q, k, 0])
            await_bytes(sx.at[q, k], cs.at[q, k, 1])
            await_bytes(sc.at[q, k], cs.at[q, k, 2])
            await_bytes(hz.at[q, k], rs.at[q, k, 0])
            await_bytes(hy.at[q, k], rs.at[q, k, 1])
            await_bytes(hy2.at[q, k], rs.at[q, k, 2])
            await_bytes(hz2.at[q, k], rs.at[q, k, 3])
            await_bytes(hz2.at[q, k], gs.at[q, k, 0])
            await_bytes(hy.at[q, k], gs.at[q, k, 1])
            await_bytes(hy2.at[q, k], gs.at[q, k, 2])
            await_bytes(hz.at[q, k], gs.at[q, k, 3])
            await_bytes(sc.at[q, k], ss.at[q, k, 0])
            await_bytes(sx.at[q, k], ss.at[q, k, 1])
            await_bytes(sz.at[q, k], ss.at[q, k, 2])
    pltpu.make_async_copy(gwi, gwi_hbm, osem.at[0]).wait()
    pltpu.make_async_copy(gwo, gwo_hbm, osem.at[1]).wait()
    for k in range(K):
        rows = pl.ds(k * RB, RB)
        pltpu.make_async_copy(gi.at[rows], gi_hbm.at[rows], osem.at[2 + k]).wait()


def shards(inputs, teacher, weight_in, weight_out):
    tokens = inputs.shape[0]
    dma = lambda *shape: pltpu.SemaphoreType.DMA(shape)
    scratch = [
        pltpu.VMEM((D, H), BF16),
        pltpu.VMEM((H, D), BF16),
        pltpu.VMEM((tokens, D), BF16),
        pltpu.VMEM((tokens, D), BF16),
        pltpu.VMEM((D, H), BF16),
        pltpu.VMEM((H, D), BF16),
        pltpu.VMEM((K, 2, RB, H), F32),
        pltpu.VMEM((2, K, 2, 2, 4, RB, H), BF16),
        pltpu.VMEM((2, K, 4, RB, H), BF16),
        pltpu.VMEM((2, K, 3, 2, RB, H), BF16),
        pltpu.VMEM((2, K, RB, H), BF16),
        pltpu.VMEM((2, K, 3, RB, H), BF16),
        pltpu.VMEM((2, K, 2, 2, 4, RB, H), BF16),
        pltpu.VMEM((2, K, 2, 2, 4, RB, D), BF16),
        pltpu.VMEM((2, K, 2, 2, 4, RB, D), BF16),
        pltpu.VMEM((2, K, 2, 4, RB, D), BF16),
        pltpu.VMEM((2, K, 3, 2, RB, D), BF16),
        pltpu.VMEM((2, K, RB, D), BF16),
        dma(K + 3), dma(2 + K),
        dma(2, K, 3), dma(2, K, 3), dma(2, K, 4), dma(2, K, 4),
        dma(2, K, 4), dma(2, K, 4), dma(2, K, 3), dma(2, K, 3),
    ]
    anywhere = pl.BlockSpec(memory_space=pl.ANY)
    return pl.pallas_call(
        kernel,
        out_shape=(
            jax.ShapeDtypeStruct((tokens, D), BF16),
            jax.ShapeDtypeStruct((D, H), BF16),
            jax.ShapeDtypeStruct((H, D), BF16),
        ),
        in_specs=[anywhere] * 4,
        out_specs=(anywhere,) * 3,
        scratch_shapes=scratch,
        compiler_params=pltpu.CompilerParams(
            collective_id=0, has_side_effects=True, vmem_limit_bytes=58 * 1024 * 1024
        ),
    )(inputs, teacher, weight_in, weight_out)


def solution(mesh):
    placed = (P("col", "row"), P("col", "row"), P("row", "col"), P("col", "row"))
    return jax.shard_map(
        shards,
        mesh=mesh,
        in_specs=placed,
        out_specs=(P("col", "row"), P("row", "col"), P("col", "row")),
        check_vma=False,
    )
```

```python
import math

import jax
import jax.numpy as jnp
from jax import lax
from jax.experimental import pallas as pl
from jax.experimental.pallas import tpu as pltpu
from jax.sharding import PartitionSpec as P

MESH = pl.DeviceIdType.MESH
F32 = jnp.float32
BF16 = jnp.bfloat16

K = 6
RB = 96 // K
D = 896
H = 1152
HALF = 8 * RB

ORDER = (
    "A0gm", "A0gc", "B0gm", "A0rs", "B0gc", "F0gm", "C0gm", "B0rs", "C0gc", "A0rB",
    "A0rC", "D0gm", "A0rE", "A0rF", "B0rB", "A0aA", "D0gc", "B0rC", "C0rs", "C0rC",
    "A0aD", "F0gc", "B0rE", "C0rB", "E0gm", "D0rs", "B0rF", "E0gc", "A0cs", "C0rF",
    "C0rE", "B0aD", "D0rB", "B0aA", "E0rs", "A0cm", "A0cz", "D0rC", "B0cs", "E0rB",
    "D0rE", "A0ce", "D0rF", "C0aA", "B0cm", "C0aD", "A1gm", "F0rs", "B0cz", "C0cs",
    "D0aA", "D0aD", "E0rC", "F0rB", "C0cm", "E0rE", "A1gc", "B0ce", "F0rC", "E0rF",
    "A1rs", "B1gm", "D0cs", "F0rE", "D0cm", "E0aA", "C0cz", "B1gc", "E0aD", "C0ce",
    "F0rF", "A1rC", "D0cz", "A1rB", "B1rs", "F0aA", "E0cs", "A1rE", "C1gm", "F0aD",
    "E0cm", "C1gc", "A1aA", "D0ce", "F0cs", "B1rB", "E0cz", "B1rC", "A1rF", "C1rs",
    "D1gm", "F0cm", "D1gc", "B1rE", "E0ce", "F0cz", "A1aD", "C1rC", "E1gm", "D1rs",
    "B1rF", "E1gc", "C1rB", "A1cs", "B1aA", "C1rF", "F0ce", "B1aD", "A1cm", "D1rB",
    "D1rC", "C1rE", "F1gm", "E1rs", "F1gc", "D1rF", "B1cs", "C1aA", "D1rE", "A1cz",
    "C1aD", "F1rs", "E1rC", "B1cm", "G", "D1aA", "B1cz", "E1rB", "D1aD", "E1rF",
    "C1cs", "E1rE", "F1rB", "B1ce", "A1ce", "F1rC", "C1cm", "E1aA", "E1aD", "D1cs",
    "F1rE", "F1rF", "E1cs", "D1cm", "F1aD", "F1aA", "E1cm", "D1cz", "F1cs", "C1cz",
    "E1cz", "F1cm", "W", "F1cz", "E1ce", "C1ce", "D1ce", "F1ce",
)


def gelu_value(hidden):
    return 0.5 * hidden * (1.0 + lax.erf(hidden * (1.0 / math.sqrt(2.0))))


def gelu_slope(hidden):
    cumul = 0.5 * (1.0 + lax.erf(hidden * (1.0 / math.sqrt(2.0))))
    return cumul + hidden * jnp.exp(-0.5 * hidden * hidden) * (1.0 / math.sqrt(2.0 * math.pi))


def kernel(
    x_hbm, t_hbm, wi_hbm, wo_hbm, gi_hbm, gwi_hbm, gwo_hbm,
    wi, wo, tch, gi, gwi, gwo, hid,
    hp, hz, hy, hz2, hy2, ag, xg, sp, sc, sx, sz,
    lsem, osem, cs, cr, rs, rr, gs, gr, ss, st,
):
    r, c = lax.axis_index("row"), lax.axis_index("col")
    zh, y = r // 4, r % 4
    zl, x, core = c // 8, c // 2 % 4, c % 2
    oz, ol, oc = 1 - zh, 1 - zl, 1 - core
    ys = [(y + j) % 4 for j in (1, 2, 3)]
    xs = [(x + j) % 4 for j in (1, 2, 3)]
    y_dev = [(zh * 4 + v, c) for v in ys]
    z_dev = (oz * 4 + y, c)
    x_dev = [(r, zl * 8 + v * 2 + core) for v in xs]
    l_dev = (r, ol * 8 + x * 2 + core)
    core_dev = (r, zl * 8 + x * 2 + oc)

    def send(src, dst, ssem, rsem, dev):
        pltpu.make_async_remote_copy(
            src_ref=src, dst_ref=dst, send_sem=ssem, recv_sem=rsem, device_id=dev, device_id_type=MESH
        ).start()

    def await_bytes(like, sem):
        pltpu.make_async_copy(like, like, sem).wait()

    loads = [pltpu.make_async_copy(x_hbm.at[pl.ds(k * RB, RB)], xg.at[0, k, core, zl, x], lsem.at[k]) for k in range(K)]
    load_wi = pltpu.make_async_copy(wi_hbm, wi, lsem.at[K])
    load_wo = pltpu.make_async_copy(wo_hbm, wo, lsem.at[K + 1])
    load_t = pltpu.make_async_copy(t_hbm, tch, lsem.at[K + 2])
    for load in loads:
        load.start()

    barrier = pltpu.get_barrier_semaphore()
    peers = y_dev + x_dev + [z_dev, l_dev, core_dev]
    for peer in peers:
        pl.semaphore_signal(barrier, inc=1, device_id=peer, device_id_type=MESH)
    pl.semaphore_wait(barrier, len(peers))

    def gather_col_start(q, k):
        own = xg.at[q, k, core, zl, x]
        send(own, own, cs.at[q, k, 0], cr.at[q, k, 0], l_dev)
        for j in (1, 0, 2):
            send(own, own, cs.at[q, k, 1], cr.at[q, k, 1], x_dev[j])

    def gather_col_mid(q, k):
        await_bytes(sz.at[q, k], cr.at[q, k, 0])
        for j in (1, 0, 2):
            got = xg.at[q, k, core, ol, x]
            send(got, got, cs.at[q, k, 1], cr.at[q, k, 1], x_dev[j])

    def gather_col_core(q, k):
        await_bytes(sx.at[q, k], cr.at[q, k, 1])
        send(xg.at[q, k, core], xg.at[q, k, core], cs.at[q, k, 2], cr.at[q, k, 2], core_dev)

    def gather_col_end(q, k):
        await_bytes(sc.at[q, k], cr.at[q, k, 2])

    def product(out, left, right, transposed):
        a = left[...].reshape(2 * HALF, left.shape[-1])
        if transposed:
            res = lax.dot_general(a, right[...], (((1,), (1,)), ((), ())), preferred_element_type=F32)
        else:
            res = jnp.dot(a, right[...], preferred_element_type=F32)
        out[...] = res.astype(BF16).reshape(out.shape)

    def row_start(q, k):
        gather_col_end(q, k)
        weights, transposed = (wi, False) if q == 0 else (wo, True)
        product(hp.at[q, k], xg.at[q, k], weights, transposed)
        send(hp.at[q, k, 1, oz], hz.at[q, k], rs.at[q, k, 0], rr.at[q, k, 0], z_dev)
        for j in (1, 0, 2):
            send(hp.at[q, k, 0, :, ys[j]], hy.at[q, k, j], rs.at[q, k, 1], rr.at[q, k, 1], y_dev[j])

    def row_after_z(q, k):
        await_bytes(hz.at[q, k], rr.at[q, k, 0])
        hp[q, k, 1, zh] = (hp[q, k, 1, zh].astype(F32) + hz[q, k].astype(F32)).astype(BF16)
        for j in (1, 0, 2):
            send(hp.at[q, k, 1, zh, ys[j]], hy2.at[q, k, j], rs.at[q, k, 2], rr.at[q, k, 2], y_dev[j])

    def row_after_y(q, k):
        await_bytes(hy.at[q, k], rr.at[q, k, 1])
        total = hp[q, k, 0, oz, y].astype(F32)
        for j in range(3):
            total = total + hy[q, k, j, oz].astype(F32)
        hp[q, k, 0, oz, y] = total.astype(BF16)
        send(hp.at[q, k, 0, oz, y], hz2.at[q, k], rs.at[q, k, 3], rr.at[q, k, 3], z_dev)

    def activate(q, k, part, total):
        if q == 0:
            hid[k, part] = total
            value = gelu_value(total)
        else:
            value = total * gelu_slope(hid[k, part])
        ag[q, k, part, zh, y] = value.astype(BF16)

    def row_end_z(q, k):
        await_bytes(hz2.at[q, k], rr.at[q, k, 3])
        total = hp[q, k, 0, zh, y].astype(F32) + hz2[q, k].astype(F32)
        for j in range(3):
            total = total + hy[q, k, j, zh].astype(F32)
        activate(q, k, 0, total)
        own = ag.at[q, k, 0, zh, y]
        send(own, own, gs.at[q, k, 0], gr.at[q, k, 0], z_dev)
        for j in (1, 0, 2):
            send(own, own, gs.at[q, k, 1], gr.at[q, k, 1], y_dev[j])

    def row_end_y(q, k):
        await_bytes(hy2.at[q, k], rr.at[q, k, 2])
        total = hp[q, k, 1, zh, y].astype(F32)
        for j in range(3):
            total = total + hy2[q, k, j].astype(F32)
        activate(q, k, 1, total)
        own = ag.at[q, k, 1, zh, y]
        for j in (1, 0, 2):
            send(own, own, gs.at[q, k, 2], gr.at[q, k, 2], y_dev[j])
        send(own, own, gs.at[q, k, 3], gr.at[q, k, 3], z_dev)

    def gather_row_z(q, k):
        await_bytes(hz2.at[q, k], gr.at[q, k, 0])
        for j in (1, 0, 2):
            got = ag.at[q, k, 0, oz, y]
            send(got, got, gs.at[q, k, 1], gr.at[q, k, 1], y_dev[j])

    def gather_row_y(q, k):
        await_bytes(hy2.at[q, k], gr.at[q, k, 2])
        for j in range(3):
            got = ag.at[q, k, 1, zh, ys[j]]
            send(got, got, gs.at[q, k, 3], gr.at[q, k, 3], z_dev)

    def col_start(q, k):
        await_bytes(hy.at[q, k], gr.at[q, k, 1])
        await_bytes(hz.at[q, k], gr.at[q, k, 3])
        weights, transposed = (wo, False) if q == 0 else (wi, True)
        product(sp.at[q, k], ag.at[q, k], weights, transposed)
        send(sp.at[q, k, oc], sc.at[q, k], ss.at[q, k, 0], st.at[q, k, 0], core_dev)

    def col_mid(q, k):
        await_bytes(sc.at[q, k], st.at[q, k, 0])
        sp[q, k, core] = (sp[q, k, core].astype(F32) + sc[q, k].astype(F32)).astype(BF16)
        for j in (1, 0, 2):
            send(sp.at[q, k, core, :, xs[j]], sx.at[q, k, j], ss.at[q, k, 1], st.at[q, k, 1], x_dev[j])

    def col_z(q, k):
        await_bytes(sx.at[q, k], st.at[q, k, 1])
        total = sp[q, k, core, ol, x].astype(F32)
        for j in range(3):
            total = total + sx[q, k, j, ol].astype(F32)
        sp[q, k, core, ol, x] = total.astype(BF16)
        send(sp.at[q, k, core, ol, x], sz.at[q, k], ss.at[q, k, 2], st.at[q, k, 2], l_dev)

    def col_end(q, k):
        await_bytes(sz.at[q, k], st.at[q, k, 2])
        total = sp[q, k, core, zl, x].astype(F32) + sz[q, k].astype(F32)
        for j in range(3):
            total = total + sx[q, k, j, zl].astype(F32)
        rows = pl.ds(k * RB, RB)
        if q == 0:
            xg[1, k, core, zl, x] = (0.125 * (total - tch[rows, :].astype(F32))).astype(BF16)
            gather_col_start(1, k)
        else:
            gi[rows, :] = total.astype(BF16)
            pltpu.make_async_copy(gi.at[rows], gi_hbm.at[rows], osem.at[2 + k]).start()

    def weight_grad(out, left, right, tile):
        b = right.reshape(K * 2 * HALF, right.shape[-1])
        a = left.reshape(K * 2 * HALF, left.shape[-1])

        def step(i, carry):
            at = pl.ds(pl.multiple_of(i * tile, tile), tile)
            out[at, :] = lax.dot_general(
                a[:, at], b[...], (((0,), (0,)), ((), ())), preferred_element_type=F32
            ).astype(BF16)
            return carry

        lax.fori_loop(0, out.shape[0] // tile, step, 0)

    for k in range(K):
        loads[k].wait()
        gather_col_start(0, k)
    load_wi.start()
    load_wo.start()
    load_t.start()

    steps = {
        "gm": gather_col_mid, "gc": gather_col_core, "rs": row_start, "rC": row_after_z, "rB": row_after_y,
        "rE": row_end_z, "rF": row_end_y, "aA": gather_row_z, "aD": gather_row_y,
        "cs": col_start, "cm": col_mid, "cz": col_z, "ce": col_end,
    }
    first = {"rs": [load_wi], "cs": [load_wo, load_t]}
    for event in ORDER:
        if event == "G":
            weight_grad(gwo, ag.at[0], xg.at[1], 384)
            pltpu.make_async_copy(gwo, gwo_hbm, osem.at[1]).start()
        elif event == "W":
            weight_grad(gwi, xg.at[0], ag.at[1], 128)
            pltpu.make_async_copy(gwi, gwi_hbm, osem.at[0]).start()
        else:
            k, q, step = ord(event[0]) - ord("A"), int(event[1]), event[2:]
            for load in first.pop(step, []):
                load.wait()
            steps[step](q, k)

    for q in range(2):
        for k in range(K):
            await_bytes(sz.at[q, k], cs.at[q, k, 0])
            await_bytes(sx.at[q, k], cs.at[q, k, 1])
            await_bytes(sc.at[q, k], cs.at[q, k, 2])
            await_bytes(hz.at[q, k], rs.at[q, k, 0])
            await_bytes(hy.at[q, k], rs.at[q, k, 1])
            await_bytes(hy2.at[q, k], rs.at[q, k, 2])
            await_bytes(hz2.at[q, k], rs.at[q, k, 3])
            await_bytes(hz2.at[q, k], gs.at[q, k, 0])
            await_bytes(hy.at[q, k], gs.at[q, k, 1])
            await_bytes(hy2.at[q, k], gs.at[q, k, 2])
            await_bytes(hz.at[q, k], gs.at[q, k, 3])
            await_bytes(sc.at[q, k], ss.at[q, k, 0])
            await_bytes(sx.at[q, k], ss.at[q, k, 1])
            await_bytes(sz.at[q, k], ss.at[q, k, 2])
    pltpu.make_async_copy(gwi, gwi_hbm, osem.at[0]).wait()
    pltpu.make_async_copy(gwo, gwo_hbm, osem.at[1]).wait()
    for k in range(K):
        rows = pl.ds(k * RB, RB)
        pltpu.make_async_copy(gi.at[rows], gi_hbm.at[rows], osem.at[2 + k]).wait()


def shards(inputs, teacher, weight_in, weight_out):
    tokens = inputs.shape[0]
    dma = lambda *shape: pltpu.SemaphoreType.DMA(shape)
    scratch = [
        pltpu.VMEM((D, H), BF16),
        pltpu.VMEM((H, D), BF16),
        pltpu.VMEM((tokens, D), BF16),
        pltpu.VMEM((tokens, D), BF16),
        pltpu.VMEM((D, H), BF16),
        pltpu.VMEM((H, D), BF16),
        pltpu.VMEM((K, 2, RB, H), F32),
        pltpu.VMEM((2, K, 2, 2, 4, RB, H), BF16),
        pltpu.VMEM((2, K, 4, RB, H), BF16),
        pltpu.VMEM((2, K, 3, 2, RB, H), BF16),
        pltpu.VMEM((2, K, RB, H), BF16),
        pltpu.VMEM((2, K, 3, RB, H), BF16),
        pltpu.VMEM((2, K, 2, 2, 4, RB, H), BF16),
        pltpu.VMEM((2, K, 2, 2, 4, RB, D), BF16),
        pltpu.VMEM((2, K, 2, 2, 4, RB, D), BF16),
        pltpu.VMEM((2, K, 2, 4, RB, D), BF16),
        pltpu.VMEM((2, K, 3, 2, RB, D), BF16),
        pltpu.VMEM((2, K, RB, D), BF16),
        dma(K + 3), dma(2 + K),
        dma(2, K, 3), dma(2, K, 3), dma(2, K, 4), dma(2, K, 4),
        dma(2, K, 4), dma(2, K, 4), dma(2, K, 3), dma(2, K, 3),
    ]
    anywhere = pl.BlockSpec(memory_space=pl.ANY)
    return pl.pallas_call(
        kernel,
        out_shape=(
            jax.ShapeDtypeStruct((tokens, D), BF16),
            jax.ShapeDtypeStruct((D, H), BF16),
            jax.ShapeDtypeStruct((H, D), BF16),
        ),
        in_specs=[anywhere] * 4,
        out_specs=(anywhere,) * 3,
        scratch_shapes=scratch,
        compiler_params=pltpu.CompilerParams(
            collective_id=0, has_side_effects=True, vmem_limit_bytes=58 * 1024 * 1024
        ),
    )(inputs, teacher, weight_in, weight_out)


def solution(mesh):
    placed = (P("col", "row"), P("col", "row"), P("row", "col"), P("col", "row"))
    return jax.shard_map(
        shards,
        mesh=mesh,
        in_specs=placed,
        out_specs=(P("col", "row"), P("row", "col"), P("col", "row")),
        check_vma=False,
    )
```

```python
import math

import jax
import jax.numpy as jnp
from jax import lax
from jax.experimental import pallas as pl
from jax.experimental.pallas import tpu as pltpu
from jax.sharding import PartitionSpec as P

MESH = pl.DeviceIdType.MESH
F32 = jnp.float32
BF16 = jnp.bfloat16

K = 6
RB = 96 // K
D = 896
H = 1152
HALF = 8 * RB
CZ = 640
CY = H - CZ

ORDER = (
    "A0gm", "A0gc", "E0gm", "D0gm", "A0rs", "C0gm", "E0gc", "D0gc", "A0rA", "B0gm",
    "C0gc", "E0rs", "A0rC", "A0rB", "C0rs", "D0rs", "A0rF", "E0rA", "E0rC", "F0gm",
    "B0gc", "B0rs", "D0rA", "A0rE", "A0aD", "D0rC", "B0rA", "C0rA", "B0rC", "D0rB",
    "A0aB", "D0rF", "F0gc", "B0rB", "D0rE", "F0rs", "B0rF", "E0rB", "B0rE", "A0cs",
    "D0aD", "F0rA", "D0aB", "B0aD", "A0cm", "E0rF", "E0rE", "B0aB", "D0cs", "C0rB",
    "C0rC", "A0cz", "E0aD", "D0cm", "F0rC", "B0cs", "F0rB", "E0aB", "A0ce", "C0rF",
    "B0cm", "D0cz", "C0rE", "E0cs", "F0rF", "A1gm", "C0aD", "D0ce", "F0rE", "B0cz",
    "E0cm", "A1gc", "F0aD", "C0aB", "D1gm", "B0ce", "F0aB", "E0cz", "C0cs", "A1rs",
    "B1gm", "D1gc", "E0ce", "C0cm", "F0cs", "B1gc", "D1rs", "F0cm", "A1rA", "B1rs",
    "C0cz", "E1gm", "D1rC", "A1rC", "B1rA", "F0cz", "E1gc", "A1rB", "C0ce", "B1rC",
    "F0ce", "E1rs", "C1gm", "A1rE", "A1rF", "F1gm", "B1rB", "C1gc", "B1rF", "E1rA",
    "F1gc", "C1rs", "F1rs", "B1rE", "E1rC", "D1rA", "E1rB", "G", "C1rA", "B1aD",
    "C1rC", "D1rB", "E1rF", "A1aB", "C1rB", "D1rF", "A1aD", "F1rA", "E1rE", "D1rE",
    "D1aD", "B1aB", "C1rF", "A1cs", "F1rB", "F1rC", "D1aB", "E1aD", "A1cm", "C1rE",
    "E1aB", "B1cs", "C1aD", "F1rF", "D1cs", "F1rE", "B1cm", "A1cz", "E1cs", "D1cm",
    "C1aB", "F1aD", "F1aB", "E1cm", "C1cs", "B1cz", "F1cs", "D1cz", "C1cm", "A1ce",
    "E1cz", "B1ce", "F1cm", "W", "C1cz", "D1ce", "F1cz", "C1ce", "E1ce", "F1ce",
)


def gelu_value(hidden):
    return 0.5 * hidden * (1.0 + lax.erf(hidden * (1.0 / math.sqrt(2.0))))


def gelu_slope(hidden):
    cumul = 0.5 * (1.0 + lax.erf(hidden * (1.0 / math.sqrt(2.0))))
    return cumul + hidden * jnp.exp(-0.5 * hidden * hidden) * (1.0 / math.sqrt(2.0 * math.pi))


def kernel(
    x_hbm, t_hbm, wi_hbm, wo_hbm, gi_hbm, gwi_hbm, gwo_hbm,
    wi, wo, tch, gi, gwi, gwo, hid_z, hid_y,
    hp, hz, hr, hy, hz2, hy2, ag, xg, sp, sc, sx, sz,
    lsem, osem, cs, cr, rs, rr, gs, gr, ss, st,
):
    r, c = lax.axis_index("row"), lax.axis_index("col")
    zh, y = r // 4, r % 4
    zl, x, core = c // 8, c // 2 % 4, c % 2
    oz, ol, oc = 1 - zh, 1 - zl, 1 - core
    ys = [(y + j) % 4 for j in (1, 2, 3)]
    xs = [(x + j) % 4 for j in (1, 2, 3)]
    y_dev = [(zh * 4 + v, c) for v in ys]
    up, across, down = ys
    up_dev, down_dev = y_dev[0], y_dev[2]
    fz, fy = pl.ds(0, CZ), pl.ds(CZ, CY)
    z_dev = (oz * 4 + y, c)
    x_dev = [(r, zl * 8 + v * 2 + core) for v in xs]
    l_dev = (r, ol * 8 + x * 2 + core)
    core_dev = (r, zl * 8 + x * 2 + oc)

    def send(src, dst, ssem, rsem, dev):
        pltpu.make_async_remote_copy(
            src_ref=src, dst_ref=dst, send_sem=ssem, recv_sem=rsem, device_id=dev, device_id_type=MESH
        ).start()

    def await_bytes(like, sem):
        pltpu.make_async_copy(like, like, sem).wait()

    loads = [pltpu.make_async_copy(x_hbm.at[pl.ds(k * RB, RB)], xg.at[0, k, core, zl, x], lsem.at[k]) for k in range(K)]
    load_wi = pltpu.make_async_copy(wi_hbm, wi, lsem.at[K])
    load_wo = pltpu.make_async_copy(wo_hbm, wo, lsem.at[K + 1])
    load_t = pltpu.make_async_copy(t_hbm, tch, lsem.at[K + 2])
    for load in loads:
        load.start()

    barrier = pltpu.get_barrier_semaphore()
    peers = y_dev + x_dev + [z_dev, l_dev, core_dev]
    for peer in peers:
        pl.semaphore_signal(barrier, inc=1, device_id=peer, device_id_type=MESH)
    pl.semaphore_wait(barrier, len(peers))

    def gather_col_start(q, k):
        own = xg.at[q, k, core, zl, x]
        send(own, own, cs.at[q, k, 0], cr.at[q, k, 0], l_dev)
        for j in (1, 0, 2):
            send(own, own, cs.at[q, k, 1], cr.at[q, k, 1], x_dev[j])

    def gather_col_mid(q, k):
        await_bytes(sz.at[q, k], cr.at[q, k, 0])
        for j in (1, 0, 2):
            got = xg.at[q, k, core, ol, x]
            send(got, got, cs.at[q, k, 1], cr.at[q, k, 1], x_dev[j])

    def gather_col_core(q, k):
        await_bytes(sx.at[q, k], cr.at[q, k, 1])
        send(xg.at[q, k, core], xg.at[q, k, core], cs.at[q, k, 2], cr.at[q, k, 2], core_dev)

    def gather_col_end(q, k):
        await_bytes(sc.at[q, k], cr.at[q, k, 2])

    def product(out, left, right, transposed):
        a = left[...].reshape(2 * HALF, left.shape[-1])
        if transposed:
            res = lax.dot_general(a, right[...], (((1,), (1,)), ((), ())), preferred_element_type=F32)
        else:
            res = jnp.dot(a, right[...], preferred_element_type=F32)
        out[...] = res.astype(BF16).reshape(out.shape)

    def row_start(q, k):
        gather_col_end(q, k)
        weights, transposed = (wi, False) if q == 0 else (wo, True)
        product(hp.at[q, k], xg.at[q, k], weights, transposed)
        part = hp.at[q, k]
        send(part.at[:, 0, across, :, fz], hr.at[q, k, 0], rs.at[q, k, 0], rr.at[q, k, 0], up_dev)
        send(part.at[:, 1, across, :, fz], hr.at[q, k, 1], rs.at[q, k, 0], rr.at[q, k, 0], down_dev)
        send(part.at[:, oz, :, :, fy], hz.at[q, k], rs.at[q, k, 3], rr.at[q, k, 3], z_dev)
        send(part.at[:, 1, up, :, fz], hy.at[q, k, 0, 1], rs.at[q, k, 1], rr.at[q, k, 1], up_dev)
        send(part.at[:, 0, down, :, fz], hy.at[q, k, 1, 0], rs.at[q, k, 1], rr.at[q, k, 1], down_dev)

    def row_relay(q, k):
        await_bytes(hr.at[q, k], rr.at[q, k, 0])
        for a, to, dev in ((0, up, up_dev), (1, down, down_dev)):
            total = hp[q, k, :, a, to, :, fz].astype(F32) + hr[q, k, a].astype(F32)
            hp[q, k, :, a, to, :, fz] = total.astype(BF16)
            send(hp.at[q, k, :, a, to, :, fz], hy.at[q, k, a, a], rs.at[q, k, 1], rr.at[q, k, 1], dev)

    def row_after_y(q, k):
        await_bytes(hy.at[q, k], rr.at[q, k, 1])
        for b in range(2):
            total = hp[q, k, :, b, y, :, fz].astype(F32)
            total = total + hy[q, k, 0, b].astype(F32) + hy[q, k, 1, b].astype(F32)
            hp[q, k, :, b, y, :, fz] = total.astype(BF16)
        send(hp.at[q, k, :, :, y, :, fz], hz2.at[q, k], rs.at[q, k, 2], rr.at[q, k, 2], z_dev)

    def row_after_z(q, k):
        await_bytes(hz.at[q, k], rr.at[q, k, 3])
        hp[q, k, :, zh, :, :, fy] = (hp[q, k, :, zh, :, :, fy].astype(F32) + hz[q, k].astype(F32)).astype(BF16)
        for j in (1, 0, 2):
            send(hp.at[q, k, :, zh, ys[j], :, fy], hy2.at[q, k, j], rs.at[q, k, 4], rr.at[q, k, 4], y_dev[j])

    def row_end_z(q, k):
        await_bytes(hz2.at[q, k], rr.at[q, k, 2])
        total = hp[q, k, :, :, y, :, fz].astype(F32) + hz2[q, k].astype(F32)
        if q == 0:
            hid_z[k] = total
            value = gelu_value(total)
        else:
            value = total * gelu_slope(hid_z[k])
        ag[q, k, :, :, y, :, fz] = value.astype(BF16)
        own = ag.at[q, k, :, :, y, :, fz]
        for dev in (up_dev, down_dev):
            send(own, own, gs.at[q, k, 0], gr.at[q, k, 0], dev)

    def row_end_y(q, k):
        await_bytes(hy2.at[q, k], rr.at[q, k, 4])
        total = hp[q, k, :, zh, y, :, fy].astype(F32)
        for j in range(3):
            total = total + hy2[q, k, j].astype(F32)
        if q == 0:
            hid_y[k] = total
            value = gelu_value(total)
        else:
            value = total * gelu_slope(hid_y[k])
        ag[q, k, :, zh, y, :, fy] = value.astype(BF16)
        own = ag.at[q, k, :, zh, y, :, fy]
        for j in (1, 0, 2):
            send(own, own, gs.at[q, k, 2], gr.at[q, k, 2], y_dev[j])
        send(own, own, gs.at[q, k, 3], gr.at[q, k, 3], z_dev)

    def gather_row_relay(q, k):
        await_bytes(hy.at[q, k], gr.at[q, k, 0])
        for a, src, dev in ((0, down, up_dev), (1, up, down_dev)):
            got = ag.at[q, k, :, a, src, :, fz]
            send(got, got, gs.at[q, k, 1], gr.at[q, k, 1], dev)

    def gather_row_y(q, k):
        await_bytes(hy2.at[q, k], gr.at[q, k, 2])
        for j in range(3):
            got = ag.at[q, k, :, zh, ys[j], :, fy]
            send(got, got, gs.at[q, k, 3], gr.at[q, k, 3], z_dev)

    def col_start(q, k):
        await_bytes(hr.at[q, k], gr.at[q, k, 1])
        await_bytes(hz.at[q, k], gr.at[q, k, 3])
        weights, transposed = (wo, False) if q == 0 else (wi, True)
        product(sp.at[q, k], ag.at[q, k], weights, transposed)
        send(sp.at[q, k, oc], sc.at[q, k], ss.at[q, k, 0], st.at[q, k, 0], core_dev)

    def col_mid(q, k):
        await_bytes(sc.at[q, k], st.at[q, k, 0])
        sp[q, k, core] = (sp[q, k, core].astype(F32) + sc[q, k].astype(F32)).astype(BF16)
        for j in (1, 0, 2):
            send(sp.at[q, k, core, :, xs[j]], sx.at[q, k, j], ss.at[q, k, 1], st.at[q, k, 1], x_dev[j])

    def col_z(q, k):
        await_bytes(sx.at[q, k], st.at[q, k, 1])
        total = sp[q, k, core, ol, x].astype(F32)
        for j in range(3):
            total = total + sx[q, k, j, ol].astype(F32)
        sp[q, k, core, ol, x] = total.astype(BF16)
        send(sp.at[q, k, core, ol, x], sz.at[q, k], ss.at[q, k, 2], st.at[q, k, 2], l_dev)

    def col_end(q, k):
        await_bytes(sz.at[q, k], st.at[q, k, 2])
        total = sp[q, k, core, zl, x].astype(F32) + sz[q, k].astype(F32)
        for j in range(3):
            total = total + sx[q, k, j, zl].astype(F32)
        rows = pl.ds(k * RB, RB)
        if q == 0:
            xg[1, k, core, zl, x] = (0.125 * (total - tch[rows, :].astype(F32))).astype(BF16)
            gather_col_start(1, k)
        else:
            gi[rows, :] = total.astype(BF16)
            pltpu.make_async_copy(gi.at[rows], gi_hbm.at[rows], osem.at[2 + k]).start()

    def weight_grad(out, left, right, tile):
        b = right.reshape(K * 2 * HALF, right.shape[-1])
        a = left.reshape(K * 2 * HALF, left.shape[-1])

        def step(i, carry):
            at = pl.ds(pl.multiple_of(i * tile, tile), tile)
            out[at, :] = lax.dot_general(
                a[:, at], b[...], (((0,), (0,)), ((), ())), preferred_element_type=F32
            ).astype(BF16)
            return carry

        lax.fori_loop(0, out.shape[0] // tile, step, 0)

    for k in range(K):
        loads[k].wait()
        gather_col_start(0, k)
    load_wi.start()
    load_wo.start()
    load_t.start()

    steps = {
        "gm": gather_col_mid, "gc": gather_col_core, "rs": row_start, "rA": row_relay, "rB": row_after_y,
        "rC": row_after_z, "rE": row_end_z, "rF": row_end_y, "aB": gather_row_relay, "aD": gather_row_y,
        "cs": col_start, "cm": col_mid, "cz": col_z, "ce": col_end,
    }
    first = {"rs": [load_wi], "cs": [load_wo, load_t]}
    for event in ORDER:
        if event == "G":
            weight_grad(gwo, ag.at[0], xg.at[1], 384)
            pltpu.make_async_copy(gwo, gwo_hbm, osem.at[1]).start()
        elif event == "W":
            weight_grad(gwi, xg.at[0], ag.at[1], 128)
            pltpu.make_async_copy(gwi, gwi_hbm, osem.at[0]).start()
        else:
            k, q, step = ord(event[0]) - ord("A"), int(event[1]), event[2:]
            for load in first.pop(step, []):
                load.wait()
            steps[step](q, k)

    for q in range(2):
        for k in range(K):
            await_bytes(sz.at[q, k], cs.at[q, k, 0])
            await_bytes(sx.at[q, k], cs.at[q, k, 1])
            await_bytes(sc.at[q, k], cs.at[q, k, 2])
            await_bytes(hr.at[q, k], rs.at[q, k, 0])
            await_bytes(hy.at[q, k], rs.at[q, k, 1])
            await_bytes(hz2.at[q, k], rs.at[q, k, 2])
            await_bytes(hz.at[q, k], rs.at[q, k, 3])
            await_bytes(hy2.at[q, k], rs.at[q, k, 4])
            await_bytes(hy.at[q, k], gs.at[q, k, 0])
            await_bytes(hr.at[q, k], gs.at[q, k, 1])
            await_bytes(hy2.at[q, k], gs.at[q, k, 2])
            await_bytes(hz.at[q, k], gs.at[q, k, 3])
            await_bytes(sc.at[q, k], ss.at[q, k, 0])
            await_bytes(sx.at[q, k], ss.at[q, k, 1])
            await_bytes(sz.at[q, k], ss.at[q, k, 2])
    pltpu.make_async_copy(gwi, gwi_hbm, osem.at[0]).wait()
    pltpu.make_async_copy(gwo, gwo_hbm, osem.at[1]).wait()
    for k in range(K):
        rows = pl.ds(k * RB, RB)
        pltpu.make_async_copy(gi.at[rows], gi_hbm.at[rows], osem.at[2 + k]).wait()


def shards(inputs, teacher, weight_in, weight_out):
    tokens = inputs.shape[0]
    dma = lambda *shape: pltpu.SemaphoreType.DMA(shape)
    scratch = [
        pltpu.VMEM((D, H), BF16),
        pltpu.VMEM((H, D), BF16),
        pltpu.VMEM((tokens, D), BF16),
        pltpu.VMEM((tokens, D), BF16),
        pltpu.VMEM((D, H), BF16),
        pltpu.VMEM((H, D), BF16),
        pltpu.VMEM((K, 2, 2, RB, CZ), F32),
        pltpu.VMEM((K, 2, RB, CY), F32),
        pltpu.VMEM((2, K, 2, 2, 4, RB, H), BF16),
        pltpu.VMEM((2, K, 2, 4, RB, CY), BF16),
        pltpu.VMEM((2, K, 2, 2, RB, CZ), BF16),
        pltpu.VMEM((2, K, 2, 2, 2, RB, CZ), BF16),
        pltpu.VMEM((2, K, 2, 2, RB, CZ), BF16),
        pltpu.VMEM((2, K, 3, 2, RB, CY), BF16),
        pltpu.VMEM((2, K, 2, 2, 4, RB, H), BF16),
        pltpu.VMEM((2, K, 2, 2, 4, RB, D), BF16),
        pltpu.VMEM((2, K, 2, 2, 4, RB, D), BF16),
        pltpu.VMEM((2, K, 2, 4, RB, D), BF16),
        pltpu.VMEM((2, K, 3, 2, RB, D), BF16),
        pltpu.VMEM((2, K, RB, D), BF16),
        dma(K + 3), dma(2 + K),
        dma(2, K, 3), dma(2, K, 3), dma(2, K, 5), dma(2, K, 5),
        dma(2, K, 4), dma(2, K, 4), dma(2, K, 3), dma(2, K, 3),
    ]
    anywhere = pl.BlockSpec(memory_space=pl.ANY)
    return pl.pallas_call(
        kernel,
        out_shape=(
            jax.ShapeDtypeStruct((tokens, D), BF16),
            jax.ShapeDtypeStruct((D, H), BF16),
            jax.ShapeDtypeStruct((H, D), BF16),
        ),
        in_specs=[anywhere] * 4,
        out_specs=(anywhere,) * 3,
        scratch_shapes=scratch,
        compiler_params=pltpu.CompilerParams(
            collective_id=0, has_side_effects=True, vmem_limit_bytes=58 * 1024 * 1024
        ),
    )(inputs, teacher, weight_in, weight_out)


def solution(mesh):
    placed = (P("col", "row"), P("col", "row"), P("row", "col"), P("col", "row"))
    return jax.shard_map(
        shards,
        mesh=mesh,
        in_specs=placed,
        out_specs=(P("col", "row"), P("row", "col"), P("col", "row")),
        check_vma=False,
    )
```

```python
import math

import jax
import jax.numpy as jnp
from jax import lax
from jax.experimental import pallas as pl
from jax.experimental.pallas import tpu as pltpu
from jax.sharding import PartitionSpec as P

MESH = pl.DeviceIdType.MESH
F32 = jnp.float32
BF16 = jnp.bfloat16

K = 6
RB = 96 // K
D = 896
H = 1152
HALF = 8 * RB
CZ = 768
CY = H - CZ

ORDER = (
    "A0gs", "E0gs", "A0gm", "B0gs", "B0gm", "A0gc", "E0gm", "B0gc", "C0gs", "A0rs",
    "E0gc", "B0rs", "E0rs", "D0gs", "C0gm", "A0rC", "F0gs", "B0rA", "B0rC", "D0gm",
    "E0rA", "C0gc", "A0rA", "B0rB", "E0rC", "D0gc", "C0rs", "D0rs", "B0rF", "F0gm",
    "B0rE", "A0rB", "A0rF", "D0rA", "B0aD", "C0rA", "E0rB", "E0rF", "A0rE", "D0rB",
    "B0aB", "A0aD", "C0rB", "F0gc", "D0rC", "E0rE", "A0aB", "B0cs", "D0rF", "F0rs",
    "C0rC", "E0aD", "A0cs", "B0cm", "E0aB", "A0cm", "C0rE", "D0aD", "C0rF", "E0cs",
    "F0rA", "A0cz", "C0aB", "B0cz", "D0rE", "E0cm", "C0aD", "A0ce", "B0ce", "F0rC",
    "F0rB", "C0cs", "D0aB", "A1gm", "B1gm", "E0cz", "F0rF", "C0cm", "F0rE", "D0cs",
    "B1gc", "E0ce", "F0aD", "D0cm", "C0cz", "A1gc", "F0aB", "B1rs", "E1gm", "C0ce",
    "A1rs", "D0cz", "F0cs", "B1rA", "E1gc", "B1rC", "C1gm", "F0cm", "A1rA", "D0ce",
    "E1rs", "C1gc", "B1rF", "A1rC", "D1gm", "C1rs", "E1rA", "D1gc", "F0cz", "A1rB",
    "E1rC", "C1rC", "D1rs", "F0ce", "C1rA", "E1rF", "B1rB", "A1rE", "A1rF", "F1gm",
    "C1rF", "C1rB", "D1rA", "B1rE", "E1rB", "F1gc", "D1rC", "C1rE", "B1aD", "F1rs",
    "D1rF", "D1rB", "B1aB", "E1rE", "A1aD", "G", "F1rA", "C1aD", "F1rC", "E1aD",
    "C1aB", "B1cs", "E1aB", "F1rB", "D1rE", "A1aB", "B1cm", "C1cs", "F1rF", "E1cs",
    "F1rE", "C1cm", "A1cs", "D1aD", "E1cm", "F1aD", "D1aB", "A1cm", "F1aB", "D1cs",
    "C1cz", "F1cs", "E1cz", "D1cm", "B1cz", "A1cz", "F1cm", "W", "D1cz", "F1cz",
    "C1ce", "A1ce", "E1ce", "B1ce", "D1ce", "F1ce",
)


def gelu_value(hidden):
    return 0.5 * hidden * (1.0 + lax.erf(hidden * (1.0 / math.sqrt(2.0))))


def gelu_slope(hidden):
    cumul = 0.5 * (1.0 + lax.erf(hidden * (1.0 / math.sqrt(2.0))))
    return cumul + hidden * jnp.exp(-0.5 * hidden * hidden) * (1.0 / math.sqrt(2.0 * math.pi))


def kernel(
    x_hbm, t_hbm, wi_hbm, wo_hbm, gi_hbm, gwi_hbm, gwo_hbm,
    wi, wo, tch, gi, gwi, gwo, hid_z, hid_y,
    hp, hz, hr, hy, hz2, hy2, ag, xg, sp, sc, sx, sz,
    lsem, osem, cs, cr, rs, rr, gs, gr, ss, st,
):
    r, c = lax.axis_index("row"), lax.axis_index("col")
    zh, y = r // 4, r % 4
    zl, x, core = c // 8, c // 2 % 4, c % 2
    oz, ol, oc = 1 - zh, 1 - zl, 1 - core
    ys = [(y + j) % 4 for j in (1, 2, 3)]
    xs = [(x + j) % 4 for j in (1, 2, 3)]
    y_dev = [(zh * 4 + v, c) for v in ys]
    up, across, down = ys
    up_dev, down_dev = y_dev[0], y_dev[2]
    fz, fy = pl.ds(0, CZ), pl.ds(CZ, CY)
    z_dev = (oz * 4 + y, c)
    x_dev = [(r, zl * 8 + v * 2 + core) for v in xs]
    l_dev = (r, ol * 8 + x * 2 + core)
    core_dev = (r, zl * 8 + x * 2 + oc)

    def send(src, dst, ssem, rsem, dev):
        pltpu.make_async_remote_copy(
            src_ref=src, dst_ref=dst, send_sem=ssem, recv_sem=rsem, device_id=dev, device_id_type=MESH
        ).start()

    def await_bytes(like, sem):
        pltpu.make_async_copy(like, like, sem).wait()

    loads = [pltpu.make_async_copy(x_hbm.at[pl.ds(k * RB, RB)], xg.at[0, k, core, zl, x], lsem.at[k]) for k in range(K)]
    load_wi = pltpu.make_async_copy(wi_hbm, wi, lsem.at[K])
    load_wo = pltpu.make_async_copy(wo_hbm, wo, lsem.at[K + 1])
    load_t = pltpu.make_async_copy(t_hbm, tch, lsem.at[K + 2])
    for load in loads:
        load.start()

    barrier = pltpu.get_barrier_semaphore()
    peers = y_dev + x_dev + [z_dev, l_dev, core_dev]
    for peer in peers:
        pl.semaphore_signal(barrier, inc=1, device_id=peer, device_id_type=MESH)
    pl.semaphore_wait(barrier, len(peers))

    def gather_col_start(q, k):
        own = xg.at[q, k, core, zl, x]
        send(own, own, cs.at[q, k, 0], cr.at[q, k, 0], l_dev)
        for j in (1, 0, 2):
            send(own, own, cs.at[q, k, 1], cr.at[q, k, 1], x_dev[j])

    def gather_col_mid(q, k):
        await_bytes(sz.at[q, k], cr.at[q, k, 0])
        for j in (1, 0, 2):
            got = xg.at[q, k, core, ol, x]
            send(got, got, cs.at[q, k, 1], cr.at[q, k, 1], x_dev[j])

    def gather_col_core(q, k):
        await_bytes(sx.at[q, k], cr.at[q, k, 1])
        send(xg.at[q, k, core], xg.at[q, k, core], cs.at[q, k, 2], cr.at[q, k, 2], core_dev)

    def gather_col_end(q, k):
        await_bytes(sc.at[q, k], cr.at[q, k, 2])

    def product(out, left, right, transposed):
        a = left[...].reshape(2 * HALF, left.shape[-1])
        if transposed:
            res = lax.dot_general(a, right[...], (((1,), (1,)), ((), ())), preferred_element_type=F32)
        else:
            res = jnp.dot(a, right[...], preferred_element_type=F32)
        out[...] = res.astype(BF16).reshape(out.shape)

    def row_start(q, k):
        gather_col_end(q, k)
        weights, transposed = (wi, False) if q == 0 else (wo, True)
        product(hp.at[q, k], xg.at[q, k], weights, transposed)
        part = hp.at[q, k]
        send(part.at[:, 0, across, :, fz], hr.at[q, k, 0], rs.at[q, k, 0], rr.at[q, k, 0], up_dev)
        send(part.at[:, 1, across, :, fz], hr.at[q, k, 1], rs.at[q, k, 0], rr.at[q, k, 0], down_dev)
        send(part.at[:, oz, :, :, fy], hz.at[q, k], rs.at[q, k, 3], rr.at[q, k, 3], z_dev)
        send(part.at[:, 1, up, :, fz], hy.at[q, k, 0, 1], rs.at[q, k, 1], rr.at[q, k, 1], up_dev)
        send(part.at[:, 0, down, :, fz], hy.at[q, k, 1, 0], rs.at[q, k, 1], rr.at[q, k, 1], down_dev)

    def row_relay(q, k):
        await_bytes(hr.at[q, k], rr.at[q, k, 0])
        for a, to, dev in ((0, up, up_dev), (1, down, down_dev)):
            total = hp[q, k, :, a, to, :, fz].astype(F32) + hr[q, k, a].astype(F32)
            hp[q, k, :, a, to, :, fz] = total.astype(BF16)
            send(hp.at[q, k, :, a, to, :, fz], hy.at[q, k, a, a], rs.at[q, k, 1], rr.at[q, k, 1], dev)

    def row_after_y(q, k):
        await_bytes(hy.at[q, k], rr.at[q, k, 1])
        for b in range(2):
            total = hp[q, k, :, b, y, :, fz].astype(F32)
            total = total + hy[q, k, 0, b].astype(F32) + hy[q, k, 1, b].astype(F32)
            hp[q, k, :, b, y, :, fz] = total.astype(BF16)
        send(hp.at[q, k, :, :, y, :, fz], hz2.at[q, k], rs.at[q, k, 2], rr.at[q, k, 2], z_dev)

    def row_after_z(q, k):
        await_bytes(hz.at[q, k], rr.at[q, k, 3])
        hp[q, k, :, zh, :, :, fy] = (hp[q, k, :, zh, :, :, fy].astype(F32) + hz[q, k].astype(F32)).astype(BF16)
        for j in (1, 0, 2):
            send(hp.at[q, k, :, zh, ys[j], :, fy], hy2.at[q, k, j], rs.at[q, k, 4], rr.at[q, k, 4], y_dev[j])

    def row_end_z(q, k):
        await_bytes(hz2.at[q, k], rr.at[q, k, 2])
        total = hp[q, k, :, :, y, :, fz].astype(F32) + hz2[q, k].astype(F32)
        if q == 0:
            hid_z[k] = total
            value = gelu_value(total)
        else:
            value = total * gelu_slope(hid_z[k])
        ag[q, k, :, :, y, :, fz] = value.astype(BF16)
        own = ag.at[q, k, :, :, y, :, fz]
        for dev in (up_dev, down_dev):
            send(own, own, gs.at[q, k, 0], gr.at[q, k, 0], dev)

    def row_end_y(q, k):
        await_bytes(hy2.at[q, k], rr.at[q, k, 4])
        total = hp[q, k, :, zh, y, :, fy].astype(F32)
        for j in range(3):
            total = total + hy2[q, k, j].astype(F32)
        if q == 0:
            hid_y[k] = total
            value = gelu_value(total)
        else:
            value = total * gelu_slope(hid_y[k])
        ag[q, k, :, zh, y, :, fy] = value.astype(BF16)
        own = ag.at[q, k, :, zh, y, :, fy]
        for j in (1, 0, 2):
            send(own, own, gs.at[q, k, 2], gr.at[q, k, 2], y_dev[j])
        send(own, own, gs.at[q, k, 3], gr.at[q, k, 3], z_dev)

    def gather_row_relay(q, k):
        await_bytes(hy.at[q, k], gr.at[q, k, 0])
        for a, src, dev in ((0, down, up_dev), (1, up, down_dev)):
            got = ag.at[q, k, :, a, src, :, fz]
            send(got, got, gs.at[q, k, 1], gr.at[q, k, 1], dev)

    def gather_row_y(q, k):
        await_bytes(hy2.at[q, k], gr.at[q, k, 2])
        for j in range(3):
            got = ag.at[q, k, :, zh, ys[j], :, fy]
            send(got, got, gs.at[q, k, 3], gr.at[q, k, 3], z_dev)

    def col_start(q, k):
        await_bytes(hr.at[q, k], gr.at[q, k, 1])
        await_bytes(hz.at[q, k], gr.at[q, k, 3])
        weights, transposed = (wo, False) if q == 0 else (wi, True)
        product(sp.at[q, k], ag.at[q, k], weights, transposed)
        send(sp.at[q, k, oc], sc.at[q, k], ss.at[q, k, 0], st.at[q, k, 0], core_dev)

    def col_mid(q, k):
        await_bytes(sc.at[q, k], st.at[q, k, 0])
        sp[q, k, core] = (sp[q, k, core].astype(F32) + sc[q, k].astype(F32)).astype(BF16)
        for j in (1, 0, 2):
            send(sp.at[q, k, core, :, xs[j]], sx.at[q, k, j], ss.at[q, k, 1], st.at[q, k, 1], x_dev[j])

    def col_z(q, k):
        await_bytes(sx.at[q, k], st.at[q, k, 1])
        total = sp[q, k, core, ol, x].astype(F32)
        for j in range(3):
            total = total + sx[q, k, j, ol].astype(F32)
        sp[q, k, core, ol, x] = total.astype(BF16)
        send(sp.at[q, k, core, ol, x], sz.at[q, k], ss.at[q, k, 2], st.at[q, k, 2], l_dev)

    def col_end(q, k):
        await_bytes(sz.at[q, k], st.at[q, k, 2])
        total = sp[q, k, core, zl, x].astype(F32) + sz[q, k].astype(F32)
        for j in range(3):
            total = total + sx[q, k, j, zl].astype(F32)
        rows = pl.ds(k * RB, RB)
        if q == 0:
            xg[1, k, core, zl, x] = (0.125 * (total - tch[rows, :].astype(F32))).astype(BF16)
            gather_col_start(1, k)
        else:
            gi[rows, :] = total.astype(BF16)
            pltpu.make_async_copy(gi.at[rows], gi_hbm.at[rows], osem.at[2 + k]).start()

    def weight_grad(out, left, right, tile):
        b = right.reshape(K * 2 * HALF, right.shape[-1])
        a = left.reshape(K * 2 * HALF, left.shape[-1])

        def step(i, carry):
            at = pl.ds(pl.multiple_of(i * tile, tile), tile)
            out[at, :] = lax.dot_general(
                a[:, at], b[...], (((0,), (0,)), ((), ())), preferred_element_type=F32
            ).astype(BF16)
            return carry

        lax.fori_loop(0, out.shape[0] // tile, step, 0)

    load_wi.start()
    load_wo.start()
    load_t.start()

    def gather_inputs(q, k):
        loads[k].wait()
        gather_col_start(q, k)

    steps = {
        "gs": gather_inputs,
        "gm": gather_col_mid, "gc": gather_col_core, "rs": row_start, "rA": row_relay, "rB": row_after_y,
        "rC": row_after_z, "rE": row_end_z, "rF": row_end_y, "aB": gather_row_relay, "aD": gather_row_y,
        "cs": col_start, "cm": col_mid, "cz": col_z, "ce": col_end,
    }
    first = {"rs": [load_wi], "cs": [load_wo, load_t]}
    for event in ORDER:
        if event == "G":
            weight_grad(gwo, ag.at[0], xg.at[1], 384)
            pltpu.make_async_copy(gwo, gwo_hbm, osem.at[1]).start()
        elif event == "W":
            weight_grad(gwi, xg.at[0], ag.at[1], 128)
            pltpu.make_async_copy(gwi, gwi_hbm, osem.at[0]).start()
        else:
            k, q, step = ord(event[0]) - ord("A"), int(event[1]), event[2:]
            for load in first.pop(step, []):
                load.wait()
            steps[step](q, k)

    for q in range(2):
        for k in range(K):
            await_bytes(sz.at[q, k], cs.at[q, k, 0])
            await_bytes(sx.at[q, k], cs.at[q, k, 1])
            await_bytes(sc.at[q, k], cs.at[q, k, 2])
            await_bytes(hr.at[q, k], rs.at[q, k, 0])
            await_bytes(hy.at[q, k], rs.at[q, k, 1])
            await_bytes(hz2.at[q, k], rs.at[q, k, 2])
            await_bytes(hz.at[q, k], rs.at[q, k, 3])
            await_bytes(hy2.at[q, k], rs.at[q, k, 4])
            await_bytes(hy.at[q, k], gs.at[q, k, 0])
            await_bytes(hr.at[q, k], gs.at[q, k, 1])
            await_bytes(hy2.at[q, k], gs.at[q, k, 2])
            await_bytes(hz.at[q, k], gs.at[q, k, 3])
            await_bytes(sc.at[q, k], ss.at[q, k, 0])
            await_bytes(sx.at[q, k], ss.at[q, k, 1])
            await_bytes(sz.at[q, k], ss.at[q, k, 2])
    pltpu.make_async_copy(gwi, gwi_hbm, osem.at[0]).wait()
    pltpu.make_async_copy(gwo, gwo_hbm, osem.at[1]).wait()
    for k in range(K):
        rows = pl.ds(k * RB, RB)
        pltpu.make_async_copy(gi.at[rows], gi_hbm.at[rows], osem.at[2 + k]).wait()


def finish(a_in, b_in, c_in, a_out, b_out, c_out, a, b, c, sem):
    moves = []
    for i, (src, mid, dst, pieces) in enumerate(((b_in, b, b_out, 4), (c_in, c, c_out, 4), (a_in, a, a_out, 1))):
        rows = src.shape[0] // pieces
        for j in range(pieces):
            at = pl.ds(j * rows, rows)
            moves.append((
                pltpu.make_async_copy(src.at[at], mid.at[at], sem.at[0, i, j]),
                pltpu.make_async_copy(mid.at[at], dst.at[at], sem.at[1, i, j]),
            ))
    for load, _ in moves:
        load.start()
    for load, store in moves:
        load.wait()
        store.start()
    for _, store in moves:
        store.wait()


def shards(inputs, teacher, weight_in, weight_out):
    tokens = inputs.shape[0]
    dma = lambda *shape: pltpu.SemaphoreType.DMA(shape)
    scratch = [
        pltpu.VMEM((D, H), BF16),
        pltpu.VMEM((H, D), BF16),
        pltpu.VMEM((tokens, D), BF16),
        pltpu.VMEM((tokens, D), BF16),
        pltpu.VMEM((D, H), BF16),
        pltpu.VMEM((H, D), BF16),
        pltpu.VMEM((K, 2, 2, RB, CZ), F32),
        pltpu.VMEM((K, 2, RB, CY), F32),
        pltpu.VMEM((2, K, 2, 2, 4, RB, H), BF16),
        pltpu.VMEM((2, K, 2, 4, RB, CY), BF16),
        pltpu.VMEM((2, K, 2, 2, RB, CZ), BF16),
        pltpu.VMEM((2, K, 2, 2, 2, RB, CZ), BF16),
        pltpu.VMEM((2, K, 2, 2, RB, CZ), BF16),
        pltpu.VMEM((2, K, 3, 2, RB, CY), BF16),
        pltpu.VMEM((2, K, 2, 2, 4, RB, H), BF16),
        pltpu.VMEM((2, K, 2, 2, 4, RB, D), BF16),
        pltpu.VMEM((2, K, 2, 2, 4, RB, D), BF16),
        pltpu.VMEM((2, K, 2, 4, RB, D), BF16),
        pltpu.VMEM((2, K, 3, 2, RB, D), BF16),
        pltpu.VMEM((2, K, RB, D), BF16),
        dma(K + 3), dma(2 + K),
        dma(2, K, 3), dma(2, K, 3), dma(2, K, 5), dma(2, K, 5),
        dma(2, K, 4), dma(2, K, 4), dma(2, K, 3), dma(2, K, 3),
    ]
    anywhere = pl.BlockSpec(memory_space=pl.ANY)
    shapes = (
        jax.ShapeDtypeStruct((tokens, D), BF16),
        jax.ShapeDtypeStruct((D, H), BF16),
        jax.ShapeDtypeStruct((H, D), BF16),
    )
    grads = pl.pallas_call(
        kernel,
        out_shape=shapes,
        in_specs=[anywhere] * 4,
        out_specs=(anywhere,) * 3,
        scratch_shapes=scratch,
        compiler_params=pltpu.CompilerParams(
            collective_id=0, has_side_effects=True, vmem_limit_bytes=58 * 1024 * 1024
        ),
    )(inputs, teacher, weight_in, weight_out)
    return pl.pallas_call(
        finish,
        out_shape=shapes,
        in_specs=[anywhere] * 3,
        out_specs=(anywhere,) * 3,
        scratch_shapes=[pltpu.VMEM(shape.shape, BF16) for shape in shapes] + [dma(2, 3, 4)],
        compiler_params=pltpu.CompilerParams(vmem_limit_bytes=58 * 1024 * 1024),
    )(*grads)


def solution(mesh):
    placed = (P("col", "row"), P("col", "row"), P("row", "col"), P("col", "row"))
    return jax.shard_map(
        shards,
        mesh=mesh,
        in_specs=placed,
        out_specs=(P("col", "row"), P("row", "col"), P("col", "row")),
        check_vma=False,
    )
```

```python
import math

import jax
import jax.numpy as jnp
from jax import lax
from jax.experimental import pallas as pl
from jax.experimental.pallas import tpu as pltpu
from jax.sharding import PartitionSpec as P

MESH = pl.DeviceIdType.MESH
F32 = jnp.float32
BF16 = jnp.bfloat16

K = 6
RB = 96 // K
D = 896
H = 1152
HALF = 8 * RB
CZ = 768
CY = H - CZ

ORDER = (
    "A0gs", "E0gs", "A0gm", "E0gm", "F0gs", "C0gs", "A0gc", "F0gm", "E0gc", "A0rs",
    "E0rs", "F0gc", "A0rA", "F0rs", "E0rA", "A0rB", "E0rC", "A0rC", "F0rA", "B0gs",
    "E0rB", "F0rC", "C0gm", "E0rF", "A0rE", "B0gm", "C0gc", "D0gs", "E0rE", "E0aD",
    "A0rF", "D0gm", "C0rs", "E0aB", "A0aB", "F0rB", "D0gc", "A0aD", "C0rA", "F0rF",
    "D0rs", "B0gc", "E0cs", "F0rE", "E0cm", "B0rs", "A0cs", "C0rB", "C0rC", "A0cm",
    "E0cz", "D0rA", "F0aD", "F0aB", "B0rA", "E0ce", "C0rF", "D0rC", "C0rE", "A0cz",
    "D0rB", "F0cs", "B0rB", "B0rC", "E1gm", "F0cm", "C0aD", "A0ce", "D0rF", "C0aB",
    "E1gc", "D0rE", "B0rE", "F0cz", "B0rF", "D0aD", "C0cs", "A1gm", "D0aB", "F0ce",
    "E1rs", "C0cm", "B0aD", "A1gc", "B0aB", "F1gm", "D0cs", "E1rC", "E1rA", "C0cz",
    "A1rs", "F1gc", "D0cm", "B0cs", "C0ce", "E1rF", "E1rB", "F1rs", "C1gm", "D0cz",
    "B0cm", "A1rA", "A1rC", "E1rE", "C1gc", "F1rA", "A1rB", "D0ce", "F1rC", "A1rF",
    "B0cz", "C1rs", "D1gm", "A1rE", "B0ce", "F1rF", "F1rB", "E1aB", "C1rA", "E1aD",
    "C1rC", "D1gc", "B1gm", "D1rs", "F1rE", "B1gc", "A1aD", "A1aB", "E1cs", "D1rA",
    "B1rs", "D1rC", "G1", "F1aD", "A1cs", "D1rB", "F1aB", "B1rA", "B1rC", "G2",
    "C1rF", "C1rB", "D1rF", "F1cs", "B1rB", "E1cm", "D1rE", "A1cm", "F1cm", "C1rE",
    "C1aD", "B1rF", "D1aD", "D1aB", "B1rE", "G0", "C1aB", "B1aD", "A1cz", "D1cs",
    "B1aB", "C1cs", "D1cm", "A1ce", "E1cz", "B1cs", "C1cm", "B1cm", "D1cz", "W0",
    "F1cz", "D1ce", "C1cz", "W2", "E1ce", "B1cz", "F1ce", "C1ce", "W1", "B1ce",
)


def gelu_value(hidden):
    return 0.5 * hidden * (1.0 + lax.erf(hidden * (1.0 / math.sqrt(2.0))))


def gelu_slope(hidden):
    cumul = 0.5 * (1.0 + lax.erf(hidden * (1.0 / math.sqrt(2.0))))
    return cumul + hidden * jnp.exp(-0.5 * hidden * hidden) * (1.0 / math.sqrt(2.0 * math.pi))


def kernel(
    x_hbm, t_hbm, wi_hbm, wo_hbm, gi_hbm, gwi_hbm, gwo_hbm,
    wi, wo, tch, gi, gwi, gwo, hid_z, hid_y,
    hp, hz, hr, hy, hz2, hy2, ag, xg, sp, sc, sx, sz,
    lsem, osem, cs, cr, rs, rr, gs, gr, ss, st,
):
    r, c = lax.axis_index("row"), lax.axis_index("col")
    zh, y = r // 4, r % 4
    zl, x, core = c // 8, c // 2 % 4, c % 2
    oz, ol, oc = 1 - zh, 1 - zl, 1 - core
    ys = [(y + j) % 4 for j in (1, 2, 3)]
    xs = [(x + j) % 4 for j in (1, 2, 3)]
    y_dev = [(zh * 4 + v, c) for v in ys]
    up, across, down = ys
    up_dev, down_dev = y_dev[0], y_dev[2]
    fz, fy = pl.ds(0, CZ), pl.ds(CZ, CY)
    z_dev = (oz * 4 + y, c)
    x_dev = [(r, zl * 8 + v * 2 + core) for v in xs]
    l_dev = (r, ol * 8 + x * 2 + core)
    core_dev = (r, zl * 8 + x * 2 + oc)

    def send(src, dst, ssem, rsem, dev):
        pltpu.make_async_remote_copy(
            src_ref=src, dst_ref=dst, send_sem=ssem, recv_sem=rsem, device_id=dev, device_id_type=MESH
        ).start()

    def await_bytes(like, sem):
        pltpu.make_async_copy(like, like, sem).wait()

    loads = [pltpu.make_async_copy(x_hbm.at[pl.ds(k * RB, RB)], xg.at[0, k, core, zl, x], lsem.at[k]) for k in range(K)]
    load_wi = pltpu.make_async_copy(wi_hbm, wi, lsem.at[K])
    load_wo = pltpu.make_async_copy(wo_hbm, wo, lsem.at[K + 1])
    load_t = pltpu.make_async_copy(t_hbm, tch, lsem.at[K + 2])
    for load in loads:
        load.start()

    barrier = pltpu.get_barrier_semaphore()
    peers = y_dev + x_dev + [z_dev, l_dev, core_dev]
    for peer in peers:
        pl.semaphore_signal(barrier, inc=1, device_id=peer, device_id_type=MESH)
    pl.semaphore_wait(barrier, len(peers))

    def gather_col_start(q, k):
        own = xg.at[q, k, core, zl, x]
        send(own, own, cs.at[q, k, 0], cr.at[q, k, 0], l_dev)
        for j in (1, 0, 2):
            send(own, own, cs.at[q, k, 1], cr.at[q, k, 1], x_dev[j])

    def gather_col_mid(q, k):
        await_bytes(sz.at[q, k], cr.at[q, k, 0])
        for j in (1, 0, 2):
            got = xg.at[q, k, core, ol, x]
            send(got, got, cs.at[q, k, 1], cr.at[q, k, 1], x_dev[j])

    def gather_col_core(q, k):
        await_bytes(sx.at[q, k], cr.at[q, k, 1])
        send(xg.at[q, k, core], xg.at[q, k, core], cs.at[q, k, 2], cr.at[q, k, 2], core_dev)

    def gather_col_end(q, k):
        await_bytes(sc.at[q, k], cr.at[q, k, 2])

    def product(out, left, right, transposed):
        a = left[...].reshape(2 * HALF, left.shape[-1])
        if transposed:
            res = lax.dot_general(a, right[...], (((1,), (1,)), ((), ())), preferred_element_type=F32)
        else:
            res = jnp.dot(a, right[...], preferred_element_type=F32)
        out[...] = res.astype(BF16).reshape(out.shape)

    def row_start(q, k):
        gather_col_end(q, k)
        weights, transposed = (wi, False) if q == 0 else (wo, True)
        product(hp.at[q, k], xg.at[q, k], weights, transposed)
        part = hp.at[q, k]
        send(part.at[:, 0, across, :, fz], hr.at[q, k, 0], rs.at[q, k, 0], rr.at[q, k, 0], up_dev)
        send(part.at[:, 1, across, :, fz], hr.at[q, k, 1], rs.at[q, k, 0], rr.at[q, k, 0], down_dev)
        send(part.at[:, oz, :, :, fy], hz.at[q, k], rs.at[q, k, 3], rr.at[q, k, 3], z_dev)
        send(part.at[:, 1, up, :, fz], hy.at[q, k, 0, 1], rs.at[q, k, 1], rr.at[q, k, 1], up_dev)
        send(part.at[:, 0, down, :, fz], hy.at[q, k, 1, 0], rs.at[q, k, 1], rr.at[q, k, 1], down_dev)

    def row_relay(q, k):
        await_bytes(hr.at[q, k], rr.at[q, k, 0])
        for a, to, dev in ((0, up, up_dev), (1, down, down_dev)):
            total = hp[q, k, :, a, to, :, fz].astype(F32) + hr[q, k, a].astype(F32)
            hp[q, k, :, a, to, :, fz] = total.astype(BF16)
            send(hp.at[q, k, :, a, to, :, fz], hy.at[q, k, a, a], rs.at[q, k, 1], rr.at[q, k, 1], dev)

    def row_after_y(q, k):
        await_bytes(hy.at[q, k], rr.at[q, k, 1])
        for b in range(2):
            total = hp[q, k, :, b, y, :, fz].astype(F32)
            total = total + hy[q, k, 0, b].astype(F32) + hy[q, k, 1, b].astype(F32)
            hp[q, k, :, b, y, :, fz] = total.astype(BF16)
        send(hp.at[q, k, :, :, y, :, fz], hz2.at[q, k], rs.at[q, k, 2], rr.at[q, k, 2], z_dev)

    def row_after_z(q, k):
        await_bytes(hz.at[q, k], rr.at[q, k, 3])
        hp[q, k, :, zh, :, :, fy] = (hp[q, k, :, zh, :, :, fy].astype(F32) + hz[q, k].astype(F32)).astype(BF16)
        for j in (1, 0, 2):
            send(hp.at[q, k, :, zh, ys[j], :, fy], hy2.at[q, k, j], rs.at[q, k, 4], rr.at[q, k, 4], y_dev[j])

    def row_end_z(q, k):
        await_bytes(hz2.at[q, k], rr.at[q, k, 2])
        total = hp[q, k, :, :, y, :, fz].astype(F32) + hz2[q, k].astype(F32)
        if q == 0:
            hid_z[k] = total
            value = gelu_value(total)
        else:
            value = total * gelu_slope(hid_z[k])
        ag[q, k, :, :, y, :, fz] = value.astype(BF16)
        own = ag.at[q, k, :, :, y, :, fz]
        for dev in (up_dev, down_dev):
            send(own, own, gs.at[q, k, 0], gr.at[q, k, 0], dev)

    def row_end_y(q, k):
        await_bytes(hy2.at[q, k], rr.at[q, k, 4])
        total = hp[q, k, :, zh, y, :, fy].astype(F32)
        for j in range(3):
            total = total + hy2[q, k, j].astype(F32)
        if q == 0:
            hid_y[k] = total
            value = gelu_value(total)
        else:
            value = total * gelu_slope(hid_y[k])
        ag[q, k, :, zh, y, :, fy] = value.astype(BF16)
        own = ag.at[q, k, :, zh, y, :, fy]
        for j in (1, 0, 2):
            send(own, own, gs.at[q, k, 2], gr.at[q, k, 2], y_dev[j])
        send(own, own, gs.at[q, k, 3], gr.at[q, k, 3], z_dev)

    def gather_row_relay(q, k):
        await_bytes(hy.at[q, k], gr.at[q, k, 0])
        for a, src, dev in ((0, down, up_dev), (1, up, down_dev)):
            got = ag.at[q, k, :, a, src, :, fz]
            send(got, got, gs.at[q, k, 1], gr.at[q, k, 1], dev)

    def gather_row_y(q, k):
        await_bytes(hy2.at[q, k], gr.at[q, k, 2])
        for j in range(3):
            got = ag.at[q, k, :, zh, ys[j], :, fy]
            send(got, got, gs.at[q, k, 3], gr.at[q, k, 3], z_dev)

    def col_start(q, k):
        await_bytes(hr.at[q, k], gr.at[q, k, 1])
        await_bytes(hz.at[q, k], gr.at[q, k, 3])
        weights, transposed = (wo, False) if q == 0 else (wi, True)
        product(sp.at[q, k], ag.at[q, k], weights, transposed)
        send(sp.at[q, k, oc], sc.at[q, k], ss.at[q, k, 0], st.at[q, k, 0], core_dev)

    def col_mid(q, k):
        await_bytes(sc.at[q, k], st.at[q, k, 0])
        sp[q, k, core] = (sp[q, k, core].astype(F32) + sc[q, k].astype(F32)).astype(BF16)
        for j in (1, 0, 2):
            send(sp.at[q, k, core, :, xs[j]], sx.at[q, k, j], ss.at[q, k, 1], st.at[q, k, 1], x_dev[j])

    def col_z(q, k):
        await_bytes(sx.at[q, k], st.at[q, k, 1])
        total = sp[q, k, core, ol, x].astype(F32)
        for j in range(3):
            total = total + sx[q, k, j, ol].astype(F32)
        sp[q, k, core, ol, x] = total.astype(BF16)
        send(sp.at[q, k, core, ol, x], sz.at[q, k], ss.at[q, k, 2], st.at[q, k, 2], l_dev)

    def col_end(q, k):
        await_bytes(sz.at[q, k], st.at[q, k, 2])
        total = sp[q, k, core, zl, x].astype(F32) + sz[q, k].astype(F32)
        for j in range(3):
            total = total + sx[q, k, j, zl].astype(F32)
        rows = pl.ds(k * RB, RB)
        if q == 0:
            xg[1, k, core, zl, x] = (0.125 * (total - tch[rows, :].astype(F32))).astype(BF16)
            gather_col_start(1, k)
        else:
            gi[rows, :] = total.astype(BF16)
            pltpu.make_async_copy(gi.at[rows], gi_hbm.at[rows], osem.at[2 + k]).start()

    def weight_grad(out, hbm, sem, left, right, tile, first, last):
        b = right.reshape(K * 2 * HALF, right.shape[-1])
        a = left.reshape(K * 2 * HALF, left.shape[-1])

        def step(i, carry):
            at = pl.ds(pl.multiple_of(i * tile, tile), tile)
            out[at, :] = lax.dot_general(
                a[:, at], b[...], (((0,), (0,)), ((), ())), preferred_element_type=F32
            ).astype(BF16)
            return carry

        lax.fori_loop(first, last, step, 0)
        rows = pl.ds(first * tile, (last - first) * tile)
        pltpu.make_async_copy(out.at[rows], hbm.at[rows], sem).start()

    load_wi.start()
    load_wo.start()
    load_t.start()

    def gather_inputs(q, k):
        loads[k].wait()
        gather_col_start(q, k)

    steps = {
        "gs": gather_inputs,
        "gm": gather_col_mid, "gc": gather_col_core, "rs": row_start, "rA": row_relay, "rB": row_after_y,
        "rC": row_after_z, "rE": row_end_z, "rF": row_end_y, "aB": gather_row_relay, "aD": gather_row_y,
        "cs": col_start, "cm": col_mid, "cz": col_z, "ce": col_end,
    }
    first = {"rs": [load_wi], "cs": [load_wo, load_t]}
    for event in ORDER:
        if event[0] == "G":
            i = int(event[1])
            weight_grad(gwo, gwo_hbm, osem.at[1], ag.at[0], xg.at[1], 384, i, i + 1)
        elif event[0] == "W":
            i = int(event[1])
            weight_grad(gwi, gwi_hbm, osem.at[0], xg.at[0], ag.at[1], 128, (0, 3, 5)[i], (3, 5, 7)[i])
        else:
            k, q, step = ord(event[0]) - ord("A"), int(event[1]), event[2:]
            for load in first.pop(step, []):
                load.wait()
            steps[step](q, k)

    for q in range(2):
        for k in range(K):
            await_bytes(sz.at[q, k], cs.at[q, k, 0])
            await_bytes(sx.at[q, k], cs.at[q, k, 1])
            await_bytes(sc.at[q, k], cs.at[q, k, 2])
            await_bytes(hr.at[q, k], rs.at[q, k, 0])
            await_bytes(hy.at[q, k], rs.at[q, k, 1])
            await_bytes(hz2.at[q, k], rs.at[q, k, 2])
            await_bytes(hz.at[q, k], rs.at[q, k, 3])
            await_bytes(hy2.at[q, k], rs.at[q, k, 4])
            await_bytes(hy.at[q, k], gs.at[q, k, 0])
            await_bytes(hr.at[q, k], gs.at[q, k, 1])
            await_bytes(hy2.at[q, k], gs.at[q, k, 2])
            await_bytes(hz.at[q, k], gs.at[q, k, 3])
            await_bytes(sc.at[q, k], ss.at[q, k, 0])
            await_bytes(sx.at[q, k], ss.at[q, k, 1])
            await_bytes(sz.at[q, k], ss.at[q, k, 2])
    pltpu.make_async_copy(gwi, gwi_hbm, osem.at[0]).wait()
    pltpu.make_async_copy(gwo, gwo_hbm, osem.at[1]).wait()
    for k in range(K):
        rows = pl.ds(k * RB, RB)
        pltpu.make_async_copy(gi.at[rows], gi_hbm.at[rows], osem.at[2 + k]).wait()


def finish(a_in, b_in, c_in, a_out, b_out, c_out, a, b, c, sem):
    moves = []
    for i, (src, mid, dst, pieces) in enumerate(((b_in, b, b_out, 4), (c_in, c, c_out, 4), (a_in, a, a_out, 1))):
        rows = src.shape[0] // pieces
        for j in range(pieces):
            at = pl.ds(j * rows, rows)
            moves.append((
                pltpu.make_async_copy(src.at[at], mid.at[at], sem.at[0, i, j]),
                pltpu.make_async_copy(mid.at[at], dst.at[at], sem.at[1, i, j]),
            ))
    for load, _ in moves:
        load.start()
    for load, store in moves:
        load.wait()
        store.start()
    for _, store in moves:
        store.wait()


def shards(inputs, teacher, weight_in, weight_out):
    tokens = inputs.shape[0]
    dma = lambda *shape: pltpu.SemaphoreType.DMA(shape)
    scratch = [
        pltpu.VMEM((D, H), BF16),
        pltpu.VMEM((H, D), BF16),
        pltpu.VMEM((tokens, D), BF16),
        pltpu.VMEM((tokens, D), BF16),
        pltpu.VMEM((D, H), BF16),
        pltpu.VMEM((H, D), BF16),
        pltpu.VMEM((K, 2, 2, RB, CZ), F32),
        pltpu.VMEM((K, 2, RB, CY), F32),
        pltpu.VMEM((2, K, 2, 2, 4, RB, H), BF16),
        pltpu.VMEM((2, K, 2, 4, RB, CY), BF16),
        pltpu.VMEM((2, K, 2, 2, RB, CZ), BF16),
        pltpu.VMEM((2, K, 2, 2, 2, RB, CZ), BF16),
        pltpu.VMEM((2, K, 2, 2, RB, CZ), BF16),
        pltpu.VMEM((2, K, 3, 2, RB, CY), BF16),
        pltpu.VMEM((2, K, 2, 2, 4, RB, H), BF16),
        pltpu.VMEM((2, K, 2, 2, 4, RB, D), BF16),
        pltpu.VMEM((2, K, 2, 2, 4, RB, D), BF16),
        pltpu.VMEM((2, K, 2, 4, RB, D), BF16),
        pltpu.VMEM((2, K, 3, 2, RB, D), BF16),
        pltpu.VMEM((2, K, RB, D), BF16),
        dma(K + 3), dma(2 + K),
        dma(2, K, 3), dma(2, K, 3), dma(2, K, 5), dma(2, K, 5),
        dma(2, K, 4), dma(2, K, 4), dma(2, K, 3), dma(2, K, 3),
    ]
    anywhere = pl.BlockSpec(memory_space=pl.ANY)
    shapes = (
        jax.ShapeDtypeStruct((tokens, D), BF16),
        jax.ShapeDtypeStruct((D, H), BF16),
        jax.ShapeDtypeStruct((H, D), BF16),
    )
    grads = pl.pallas_call(
        kernel,
        out_shape=shapes,
        in_specs=[anywhere] * 4,
        out_specs=(anywhere,) * 3,
        scratch_shapes=scratch,
        compiler_params=pltpu.CompilerParams(
            collective_id=0, has_side_effects=True, vmem_limit_bytes=58 * 1024 * 1024
        ),
    )(inputs, teacher, weight_in, weight_out)
    return pl.pallas_call(
        finish,
        out_shape=shapes,
        in_specs=[anywhere] * 3,
        out_specs=(anywhere,) * 3,
        scratch_shapes=[pltpu.VMEM(shape.shape, BF16) for shape in shapes] + [dma(2, 3, 4)],
        compiler_params=pltpu.CompilerParams(vmem_limit_bytes=58 * 1024 * 1024),
    )(*grads)


def solution(mesh):
    placed = (P("col", "row"), P("col", "row"), P("row", "col"), P("col", "row"))
    return jax.shard_map(
        shards,
        mesh=mesh,
        in_specs=placed,
        out_specs=(P("col", "row"), P("row", "col"), P("col", "row")),
        check_vma=False,
    )
```

```python
import math

import jax
import jax.numpy as jnp
from jax import lax
from jax.experimental import pallas as pl
from jax.experimental.pallas import tpu as pltpu
from jax.sharding import PartitionSpec as P

MESH = pl.DeviceIdType.MESH
F32 = jnp.float32
BF16 = jnp.bfloat16

K = 6
RB = 96 // K
D = 896
H = 1152
HALF = 8 * RB
CZ = 640
CY = H - CZ

ORDER = (
    "E0gs", "C0gs", "E0gm", "C0gm", "B0gs", "E0gc", "B0gm", "C0gc", "A0gs", "F0gs",
    "D0gs", "E0rs", "B0gc", "C0rs", "E0rA", "B0rs", "D0gm", "E0rC", "C0rA", "A0gm",
    "B0rA", "F0gm", "C0rC", "E0rB", "E0rF", "D0gc", "B0rB", "B0rC", "A0gc", "C0rB",
    "E0rE", "C0rF", "E0aD", "B0rF", "E0aB", "B0rE", "A0rs", "B0aD", "C0rE", "E0cs",
    "B0aB", "C0aD", "D0rs", "A0rA", "F0gc", "E0cm", "C0aB", "A0rC", "F0rs", "B0cs",
    "E0cz", "D0rA", "C0cs", "A0rB", "B0cm", "A0rF", "F0rA", "D0rC", "F0rC", "E0ce",
    "C0cm", "D0rB", "A0rE", "B0cz", "A0aD", "D0rF", "E1gm", "B0ce", "D0rE", "C0cz",
    "F0rB", "A0aB", "F0rF", "E1gc", "B1gm", "C0ce", "D0aD", "D0aB", "E1rs", "A0cs",
    "B1gc", "C1gm", "F0aD", "F0rE", "D0cs", "E1rA", "A0cm", "B1rs", "C1gc", "F0aB",
    "E1rC", "D0cm", "C1rs", "A0cz", "F0cs", "B1rA", "B1rC", "D0cz", "E1rF", "E1rB",
    "C1rA", "F0cm", "C1rC", "A0ce", "D0ce", "B1rB", "B1rF", "E1rE", "A1gm", "F0cz",
    "D1gm", "C1rB", "C1rF", "B1rE", "A1gc", "F0ce", "E1aB", "E1aD", "C1rE", "D1gc",
    "A1rs", "F1gm", "D1rs", "C1aD", "E1cs", "F1gc", "A1rA", "C1aB", "B1aB", "A1rC",
    "A1rB", "E1cm", "D1rA", "F1rs", "D1rC", "A1rF", "G1", "D1rB", "F1rA", "C1cs",
    "A1rE", "B1aD", "F1rC", "F1rB", "A1aD", "D1rE", "D1rF", "G0", "A1aB", "B1cs",
    "F1rF", "C1cm", "F1rE", "D1aB", "E1cz", "D1aD", "B1cm", "A1cs", "F1aD", "F1aB",
    "A1cm", "D1cs", "G2", "F1cs", "D1cm", "W1", "F1cm", "A1cz", "W2", "C1cz",
    "D1cz", "B1cz", "W0", "F1cz", "A1ce", "B1ce", "C1ce", "E1ce", "D1ce", "F1ce",
)


def gelu_value(hidden):
    return 0.5 * hidden * (1.0 + lax.erf(hidden * (1.0 / math.sqrt(2.0))))


def gelu_slope(hidden):
    cumul = 0.5 * (1.0 + lax.erf(hidden * (1.0 / math.sqrt(2.0))))
    return cumul + hidden * jnp.exp(-0.5 * hidden * hidden) * (1.0 / math.sqrt(2.0 * math.pi))


def kernel(
    x_hbm, t_hbm, wi_hbm, wo_hbm, gi_hbm, gwi_hbm, gwo_hbm,
    wi, wo, tch, gi, gwi, gwo, hid_z, hid_y,
    hp, hz, hr, hy, hz2, hy2, ag, xg, sp, sc, sx, sz,
    lsem, osem, cs, cr, rs, rr, gs, gr, ss, st,
):
    r, c = lax.axis_index("row"), lax.axis_index("col")
    zh, y = r // 4, r % 4
    zl, x, core = c // 8, c // 2 % 4, c % 2
    oz, ol, oc = 1 - zh, 1 - zl, 1 - core
    ys = [(y + j) % 4 for j in (1, 2, 3)]
    xs = [(x + j) % 4 for j in (1, 2, 3)]
    y_dev = [(zh * 4 + v, c) for v in ys]
    up, across, down = ys
    up_dev, down_dev = y_dev[0], y_dev[2]
    fz, fy = pl.ds(0, CZ), pl.ds(CZ, CY)
    z_dev = (oz * 4 + y, c)
    x_dev = [(r, zl * 8 + v * 2 + core) for v in xs]
    l_dev = (r, ol * 8 + x * 2 + core)
    core_dev = (r, zl * 8 + x * 2 + oc)

    def send(src, dst, ssem, rsem, dev):
        pltpu.make_async_remote_copy(
            src_ref=src, dst_ref=dst, send_sem=ssem, recv_sem=rsem, device_id=dev, device_id_type=MESH
        ).start()

    def await_bytes(like, sem):
        pltpu.make_async_copy(like, like, sem).wait()

    loads = [pltpu.make_async_copy(x_hbm.at[pl.ds(k * RB, RB)], xg.at[0, k, core, zl, x], lsem.at[k]) for k in range(K)]
    load_wi = pltpu.make_async_copy(wi_hbm, wi, lsem.at[K])
    load_wo = pltpu.make_async_copy(wo_hbm, wo, lsem.at[K + 1])
    load_t = pltpu.make_async_copy(t_hbm, tch, lsem.at[K + 2])
    for load in loads:
        load.start()

    barrier = pltpu.get_barrier_semaphore()
    peers = y_dev + x_dev + [z_dev, l_dev, core_dev]
    for peer in peers:
        pl.semaphore_signal(barrier, inc=1, device_id=peer, device_id_type=MESH)
    pl.semaphore_wait(barrier, len(peers))

    def gather_col_start(q, k):
        own = xg.at[q, k, core, zl, x]
        send(own, own, cs.at[q, k, 0], cr.at[q, k, 0], l_dev)
        for j in (1, 0, 2):
            send(own, own, cs.at[q, k, 1], cr.at[q, k, 1], x_dev[j])

    def gather_col_mid(q, k):
        await_bytes(sz.at[q, k], cr.at[q, k, 0])
        for j in (1, 0, 2):
            got = xg.at[q, k, core, ol, x]
            send(got, got, cs.at[q, k, 1], cr.at[q, k, 1], x_dev[j])

    def gather_col_core(q, k):
        await_bytes(sx.at[q, k], cr.at[q, k, 1])
        send(xg.at[q, k, core], xg.at[q, k, core], cs.at[q, k, 2], cr.at[q, k, 2], core_dev)

    def gather_col_end(q, k):
        await_bytes(sc.at[q, k], cr.at[q, k, 2])

    def product(out, left, right, transposed):
        a = left[...].reshape(2 * HALF, left.shape[-1])
        if transposed:
            res = lax.dot_general(a, right[...], (((1,), (1,)), ((), ())), preferred_element_type=F32)
        else:
            res = jnp.dot(a, right[...], preferred_element_type=F32)
        out[...] = res.astype(BF16).reshape(out.shape)

    def row_start(q, k):
        gather_col_end(q, k)
        weights, transposed = (wi, False) if q == 0 else (wo, True)
        product(hp.at[q, k], xg.at[q, k], weights, transposed)
        part = hp.at[q, k]
        send(part.at[:, 0, across, :, fz], hr.at[q, k, 0], rs.at[q, k, 0], rr.at[q, k, 0], up_dev)
        send(part.at[:, 1, across, :, fz], hr.at[q, k, 1], rs.at[q, k, 0], rr.at[q, k, 0], down_dev)
        send(part.at[:, oz, :, :, fy], hz.at[q, k], rs.at[q, k, 3], rr.at[q, k, 3], z_dev)
        send(part.at[:, 1, up, :, fz], hy.at[q, k, 0, 1], rs.at[q, k, 1], rr.at[q, k, 1], up_dev)
        send(part.at[:, 0, down, :, fz], hy.at[q, k, 1, 0], rs.at[q, k, 1], rr.at[q, k, 1], down_dev)

    def row_relay(q, k):
        await_bytes(hr.at[q, k], rr.at[q, k, 0])
        for a, to, dev in ((0, up, up_dev), (1, down, down_dev)):
            total = hp[q, k, :, a, to, :, fz].astype(F32) + hr[q, k, a].astype(F32)
            hp[q, k, :, a, to, :, fz] = total.astype(BF16)
            send(hp.at[q, k, :, a, to, :, fz], hy.at[q, k, a, a], rs.at[q, k, 1], rr.at[q, k, 1], dev)

    def row_after_y(q, k):
        await_bytes(hy.at[q, k], rr.at[q, k, 1])
        for b in range(2):
            total = hp[q, k, :, b, y, :, fz].astype(F32)
            total = total + hy[q, k, 0, b].astype(F32) + hy[q, k, 1, b].astype(F32)
            hp[q, k, :, b, y, :, fz] = total.astype(BF16)
        send(hp.at[q, k, :, :, y, :, fz], hz2.at[q, k], rs.at[q, k, 2], rr.at[q, k, 2], z_dev)

    def row_after_z(q, k):
        await_bytes(hz.at[q, k], rr.at[q, k, 3])
        hp[q, k, :, zh, :, :, fy] = (hp[q, k, :, zh, :, :, fy].astype(F32) + hz[q, k].astype(F32)).astype(BF16)
        for j in (1, 0, 2):
            send(hp.at[q, k, :, zh, ys[j], :, fy], hy2.at[q, k, j], rs.at[q, k, 4], rr.at[q, k, 4], y_dev[j])

    def row_end_z(q, k):
        await_bytes(hz2.at[q, k], rr.at[q, k, 2])
        total = hp[q, k, :, :, y, :, fz].astype(F32) + hz2[q, k].astype(F32)
        if q == 0:
            hid_z[k] = total
            value = gelu_value(total)
        else:
            value = total * gelu_slope(hid_z[k])
        ag[q, k, :, :, y, :, fz] = value.astype(BF16)
        own = ag.at[q, k, :, :, y, :, fz]
        for dev in (up_dev, down_dev):
            send(own, own, gs.at[q, k, 0], gr.at[q, k, 0], dev)

    def row_end_y(q, k):
        await_bytes(hy2.at[q, k], rr.at[q, k, 4])
        total = hp[q, k, :, zh, y, :, fy].astype(F32)
        for j in range(3):
            total = total + hy2[q, k, j].astype(F32)
        if q == 0:
            hid_y[k] = total
            value = gelu_value(total)
        else:
            value = total * gelu_slope(hid_y[k])
        ag[q, k, :, zh, y, :, fy] = value.astype(BF16)
        own = ag.at[q, k, :, zh, y, :, fy]
        for j in (1, 0, 2):
            send(own, own, gs.at[q, k, 2], gr.at[q, k, 2], y_dev[j])
        send(own, own, gs.at[q, k, 3], gr.at[q, k, 3], z_dev)

    def gather_row_relay(q, k):
        await_bytes(hy.at[q, k], gr.at[q, k, 0])
        for a, src, dev in ((0, down, up_dev), (1, up, down_dev)):
            got = ag.at[q, k, :, a, src, :, fz]
            send(got, got, gs.at[q, k, 1], gr.at[q, k, 1], dev)

    def gather_row_y(q, k):
        await_bytes(hy2.at[q, k], gr.at[q, k, 2])
        for j in range(3):
            got = ag.at[q, k, :, zh, ys[j], :, fy]
            send(got, got, gs.at[q, k, 3], gr.at[q, k, 3], z_dev)

    def col_start(q, k):
        await_bytes(hr.at[q, k], gr.at[q, k, 1])
        await_bytes(hz.at[q, k], gr.at[q, k, 3])
        weights, transposed = (wo, False) if q == 0 else (wi, True)
        product(sp.at[q, k], ag.at[q, k], weights, transposed)
        send(sp.at[q, k, oc], sc.at[q, k], ss.at[q, k, 0], st.at[q, k, 0], core_dev)

    def col_mid(q, k):
        await_bytes(sc.at[q, k], st.at[q, k, 0])
        sp[q, k, core] = (sp[q, k, core].astype(F32) + sc[q, k].astype(F32)).astype(BF16)
        for j in (1, 0, 2):
            send(sp.at[q, k, core, :, xs[j]], sx.at[q, k, j], ss.at[q, k, 1], st.at[q, k, 1], x_dev[j])

    def col_z(q, k):
        await_bytes(sx.at[q, k], st.at[q, k, 1])
        total = sp[q, k, core, ol, x].astype(F32)
        for j in range(3):
            total = total + sx[q, k, j, ol].astype(F32)
        sp[q, k, core, ol, x] = total.astype(BF16)
        send(sp.at[q, k, core, ol, x], sz.at[q, k], ss.at[q, k, 2], st.at[q, k, 2], l_dev)

    def col_end(q, k):
        await_bytes(sz.at[q, k], st.at[q, k, 2])
        total = sp[q, k, core, zl, x].astype(F32) + sz[q, k].astype(F32)
        for j in range(3):
            total = total + sx[q, k, j, zl].astype(F32)
        rows = pl.ds(k * RB, RB)
        if q == 0:
            xg[1, k, core, zl, x] = (0.125 * (total - tch[rows, :].astype(F32))).astype(BF16)
            gather_col_start(1, k)
        else:
            gi[rows, :] = total.astype(BF16)
            pltpu.make_async_copy(gi.at[rows], gi_hbm.at[rows], osem.at[2 + k]).start()

    def weight_grad(out, hbm, sem, left, right, tile, first, last):
        b = right.reshape(K * 2 * HALF, right.shape[-1])
        a = left.reshape(K * 2 * HALF, left.shape[-1])

        def step(i, carry):
            at = pl.ds(pl.multiple_of(i * tile, tile), tile)
            out[at, :] = lax.dot_general(
                a[:, at], b[...], (((0,), (0,)), ((), ())), preferred_element_type=F32
            ).astype(BF16)
            return carry

        lax.fori_loop(first, last, step, 0)
        rows = pl.ds(first * tile, (last - first) * tile)
        pltpu.make_async_copy(out.at[rows], hbm.at[rows], sem).start()

    load_wi.start()
    load_wo.start()
    load_t.start()

    def gather_inputs(q, k):
        loads[k].wait()
        gather_col_start(q, k)

    steps = {
        "gs": gather_inputs,
        "gm": gather_col_mid, "gc": gather_col_core, "rs": row_start, "rA": row_relay, "rB": row_after_y,
        "rC": row_after_z, "rE": row_end_z, "rF": row_end_y, "aB": gather_row_relay, "aD": gather_row_y,
        "cs": col_start, "cm": col_mid, "cz": col_z, "ce": col_end,
    }
    first = {"rs": [load_wi], "cs": [load_wo, load_t]}
    for event in ORDER:
        if event[0] == "G":
            i = int(event[1])
            weight_grad(gwo, gwo_hbm, osem.at[1], ag.at[0], xg.at[1], 384, i, i + 1)
        elif event[0] == "W":
            i = int(event[1])
            weight_grad(gwi, gwi_hbm, osem.at[0], xg.at[0], ag.at[1], 128, (0, 3, 5)[i], (3, 5, 7)[i])
        else:
            k, q, step = ord(event[0]) - ord("A"), int(event[1]), event[2:]
            for load in first.pop(step, []):
                load.wait()
            steps[step](q, k)

    for q in range(2):
        for k in range(K):
            await_bytes(sz.at[q, k], cs.at[q, k, 0])
            await_bytes(sx.at[q, k], cs.at[q, k, 1])
            await_bytes(sc.at[q, k], cs.at[q, k, 2])
            await_bytes(hr.at[q, k], rs.at[q, k, 0])
            await_bytes(hy.at[q, k], rs.at[q, k, 1])
            await_bytes(hz2.at[q, k], rs.at[q, k, 2])
            await_bytes(hz.at[q, k], rs.at[q, k, 3])
            await_bytes(hy2.at[q, k], rs.at[q, k, 4])
            await_bytes(hy.at[q, k], gs.at[q, k, 0])
            await_bytes(hr.at[q, k], gs.at[q, k, 1])
            await_bytes(hy2.at[q, k], gs.at[q, k, 2])
            await_bytes(hz.at[q, k], gs.at[q, k, 3])
            await_bytes(sc.at[q, k], ss.at[q, k, 0])
            await_bytes(sx.at[q, k], ss.at[q, k, 1])
            await_bytes(sz.at[q, k], ss.at[q, k, 2])
    pltpu.make_async_copy(gwi, gwi_hbm, osem.at[0]).wait()
    pltpu.make_async_copy(gwo, gwo_hbm, osem.at[1]).wait()
    for k in range(K):
        rows = pl.ds(k * RB, RB)
        pltpu.make_async_copy(gi.at[rows], gi_hbm.at[rows], osem.at[2 + k]).wait()


def finish(a_in, b_in, c_in, a_out, b_out, c_out, a, b, c, sem):
    moves = []
    for i, (src, mid, dst, pieces) in enumerate(((b_in, b, b_out, 4), (c_in, c, c_out, 4), (a_in, a, a_out, 1))):
        rows = src.shape[0] // pieces
        for j in range(pieces):
            at = pl.ds(j * rows, rows)
            moves.append((
                pltpu.make_async_copy(src.at[at], mid.at[at], sem.at[0, i, j]),
                pltpu.make_async_copy(mid.at[at], dst.at[at], sem.at[1, i, j]),
            ))
    for load, _ in moves:
        load.start()
    for load, store in moves:
        load.wait()
        store.start()
    for _, store in moves:
        store.wait()


def shards(inputs, teacher, weight_in, weight_out):
    tokens = inputs.shape[0]
    dma = lambda *shape: pltpu.SemaphoreType.DMA(shape)
    scratch = [
        pltpu.VMEM((D, H), BF16),
        pltpu.VMEM((H, D), BF16),
        pltpu.VMEM((tokens, D), BF16),
        pltpu.VMEM((tokens, D), BF16),
        pltpu.VMEM((D, H), BF16),
        pltpu.VMEM((H, D), BF16),
        pltpu.VMEM((K, 2, 2, RB, CZ), F32),
        pltpu.VMEM((K, 2, RB, CY), F32),
        pltpu.VMEM((2, K, 2, 2, 4, RB, H), BF16),
        pltpu.VMEM((2, K, 2, 4, RB, CY), BF16),
        pltpu.VMEM((2, K, 2, 2, RB, CZ), BF16),
        pltpu.VMEM((2, K, 2, 2, 2, RB, CZ), BF16),
        pltpu.VMEM((2, K, 2, 2, RB, CZ), BF16),
        pltpu.VMEM((2, K, 3, 2, RB, CY), BF16),
        pltpu.VMEM((2, K, 2, 2, 4, RB, H), BF16),
        pltpu.VMEM((2, K, 2, 2, 4, RB, D), BF16),
        pltpu.VMEM((2, K, 2, 2, 4, RB, D), BF16),
        pltpu.VMEM((2, K, 2, 4, RB, D), BF16),
        pltpu.VMEM((2, K, 3, 2, RB, D), BF16),
        pltpu.VMEM((2, K, RB, D), BF16),
        dma(K + 3), dma(2 + K),
        dma(2, K, 3), dma(2, K, 3), dma(2, K, 5), dma(2, K, 5),
        dma(2, K, 4), dma(2, K, 4), dma(2, K, 3), dma(2, K, 3),
    ]
    anywhere = pl.BlockSpec(memory_space=pl.ANY)
    shapes = (
        jax.ShapeDtypeStruct((tokens, D), BF16),
        jax.ShapeDtypeStruct((D, H), BF16),
        jax.ShapeDtypeStruct((H, D), BF16),
    )
    grads = pl.pallas_call(
        kernel,
        out_shape=shapes,
        in_specs=[anywhere] * 4,
        out_specs=(anywhere,) * 3,
        scratch_shapes=scratch,
        compiler_params=pltpu.CompilerParams(
            collective_id=0, has_side_effects=True, vmem_limit_bytes=58 * 1024 * 1024
        ),
    )(inputs, teacher, weight_in, weight_out)
    return pl.pallas_call(
        finish,
        out_shape=shapes,
        in_specs=[anywhere] * 3,
        out_specs=(anywhere,) * 3,
        scratch_shapes=[pltpu.VMEM(shape.shape, BF16) for shape in shapes] + [dma(2, 3, 4)],
        compiler_params=pltpu.CompilerParams(vmem_limit_bytes=58 * 1024 * 1024),
    )(*grads)


def solution(mesh):
    placed = (P("col", "row"), P("col", "row"), P("row", "col"), P("col", "row"))
    return jax.shard_map(
        shards,
        mesh=mesh,
        in_specs=placed,
        out_specs=(P("col", "row"), P("row", "col"), P("col", "row")),
        check_vma=False,
    )
```
